128 devices in a mesh: dp: 16 (over y_lo, z, core), feat: 8 (over x, y_hi).
Axes of the slice: x: 4, y: 4 (y_hi: 2, y_lo: 2; y = y_hi * 2 + y_lo), z: 4, core: 2. Of those that a mesh axis runs over, the one named last changes fastest.
Arguments:
- emb_a: bfloat16 [2048, 1536], P('dp'), may hold values from -6 to 6
- emb_b: bfloat16 [2048, 1536], P('dp'), may hold values from -6 to 6
- w_in: bfloat16 [1536, 8192], P(None, 'feat'), may hold values from -0.15625 to 0.15625
- w_out: bfloat16 [8192, 8192], P(None, 'feat'), may hold values from -0.0625 to 0.0625
- gain: float32 [8192], P('feat'), may hold values from 0.5 to 1.5
- shift: float32 [8192], P('feat'), may hold values from -3 to 3
Outputs:
- grad_in: float32 [1536, 8192], P('dp', 'feat')
- grad_gain: float32 [8192], P('feat')
- grad_shift: float32 [8192], P('feat')
- diag_loss: float32 [8192], P('feat')
- row_loss: float32 [2048], P('dp')
The draws below stay inside these ranges and needn't reach their ends.
All inputs are finite; a program needn't handle non-finite values.
Results may differ from the reference program's by a relative error of at most 0.019.
Values may be sent and summed in bfloat16 or wider, within the bound.
A program may use at most 128 MiB of HBM per device.

```python
import jax
import jax.numpy as jnp
from jax import lax

E = 1536
F = 8192
BATCH = 2048


def shard_levels(own_key, dims, pieces, least, largest):
    factor_of = 1.0
    for dim, blocks in pieces:
        heights = jax.random.uniform(jax.random.fold_in(jax.random.fold_in(own_key, 6), dim), (blocks,), jnp.float32, least / len(pieces), largest / len(pieces))
        factor_of = factor_of * jnp.repeat(jnp.exp(heights), dims[dim] // blocks).reshape((-1,) + (1,) * (len(dims) - 1 - dim))
    return factor_of


def gaussian(rng, extent, scale, bound, split=(), kind=jnp.bfloat16):
    loudness = shard_levels(rng, extent, split, -0.22, 0.18) if split else 1.0
    drawn = jax.random.normal(rng, extent, jnp.float32) * scale * loudness
    return jnp.minimum(jnp.maximum(drawn, -bound), bound).astype(kind)


def setup_inputs(seed: int = 0) -> dict:
    arg_keys = jax.random.split(jax.random.key(seed), 7)
    return {
        "emb_a": gaussian(arg_keys[0], (BATCH, E), 1.0, 6.0, ((0, 16),)),
        "emb_b": gaussian(arg_keys[1], (BATCH, E), 1.0, 6.0, ((0, 16),)),
        "w_in": gaussian(arg_keys[2], (E, F), E ** -0.5, 0.15625, ((1, 8),)),
        "w_out": gaussian(arg_keys[3], (F, F), F ** -0.5, 0.0625, ((1, 8),)),
        "gain": jnp.clip(1.0 + 0.1 * jax.random.normal(arg_keys[4], (F,), jnp.float32), 0.5, 1.5),
        "shift": gaussian(arg_keys[5], (F,), 0.5, 3.0, ((0, 8),), jnp.float32),
    }


epsilon = 1e-05
off_weight = 0.0051

def moments(values):
    center = lax.optimization_barrier(jnp.mean(values, axis=0))
    spread = lax.optimization_barrier(jnp.mean((values - center) ** 2, axis=0))
    return (center, lax.rsqrt(spread + epsilon))

def forward(embedded, w_in, w_out, gain, shift):
    hidden = jnp.dot(embedded, w_in, preferred_element_type=jnp.float32)
    center, inverse = moments(hidden)
    first_hat = (hidden - center) * inverse
    before = gain * first_hat + shift
    active = jnp.maximum(before, 0.0).astype(jnp.bfloat16)
    output = jnp.dot(active, w_out, preferred_element_type=jnp.float32)
    center_out, inverse_out = moments(output)
    second_hat = (output - center_out) * inverse_out
    return (first_hat, inverse, before, second_hat, inverse_out, second_hat.astype(jnp.bfloat16))

def norm_back(upstream, normed, inverse):
    return inverse * (upstream - lax.optimization_barrier(jnp.mean(upstream, axis=0)) - normed * lax.optimization_barrier(jnp.mean(upstream * normed, axis=0)))

def reference(emb_a, emb_b, w_in, w_out, gain, shift):
    batch = emb_a.shape[0]
    width = w_out.shape[0]
    hat_a, inv_a, pre_a, out_a, oinv_a, norm_a = forward(emb_a, w_in, w_out, gain, shift)
    hat_b, inv_b, pre_b, out_b, oinv_b, norm_b = forward(emb_b, w_in, w_out, gain, shift)
    corr_diag = lax.optimization_barrier(jnp.sum(norm_a.astype(jnp.float32) * norm_b.astype(jnp.float32), axis=0)) / batch
    gram_a = jnp.dot(norm_a, norm_a.T, preferred_element_type=jnp.float32)
    gram_b = jnp.dot(norm_b, norm_b.T, preferred_element_type=jnp.float32)
    diag_loss = (1.0 - corr_diag) ** 2 - off_weight * corr_diag ** 2
    row_loss = lax.optimization_barrier(jnp.sum(gram_a * gram_b, axis=1)) / (batch * width)
    factor = batch / 64.0
    column = -2.0 * (1.0 - corr_diag) - 2.0 * off_weight * corr_diag
    coeff = 2.0 * off_weight / (batch * batch)
    grad_norm_a = factor * (coeff * jnp.dot(gram_b.astype(jnp.bfloat16), norm_a, preferred_element_type=jnp.float32) + norm_b.astype(jnp.float32) * column / batch)
    grad_norm_b = factor * (coeff * jnp.dot(gram_a.astype(jnp.bfloat16), norm_b, preferred_element_type=jnp.float32) + norm_a.astype(jnp.float32) * column / batch)
    grad_out_a = norm_back(grad_norm_a, out_a, oinv_a).astype(jnp.bfloat16)
    grad_out_b = norm_back(grad_norm_b, out_b, oinv_b).astype(jnp.bfloat16)
    grad_act_a = jnp.dot(grad_out_a, w_out.T, preferred_element_type=jnp.float32)
    grad_act_b = jnp.dot(grad_out_b, w_out.T, preferred_element_type=jnp.float32)
    grad_pre_a = jnp.where(pre_a > 0, grad_act_a, 0.0)
    grad_pre_b = jnp.where(pre_b > 0, grad_act_b, 0.0)
    grad_shift = lax.optimization_barrier(jnp.sum(grad_pre_a, axis=0)) + lax.optimization_barrier(jnp.sum(grad_pre_b, axis=0))
    grad_gain = lax.optimization_barrier(jnp.sum(grad_pre_a * hat_a, axis=0)) + lax.optimization_barrier(jnp.sum(grad_pre_b * hat_b, axis=0))
    grad_hid_a = (gain * norm_back(grad_pre_a, hat_a, inv_a)).astype(jnp.bfloat16)
    grad_hid_b = (gain * norm_back(grad_pre_b, hat_b, inv_b)).astype(jnp.bfloat16)
    grad_in = jnp.dot(emb_a.T, grad_hid_a, preferred_element_type=jnp.float32) + jnp.dot(emb_b.T, grad_hid_b, preferred_element_type=jnp.float32)
    return (grad_in, grad_gain, grad_shift, diag_loss, row_loss)
```

```python
import functools

import jax
import jax.numpy as jnp
from jax import lax
from jax.experimental import pallas as pl
from jax.experimental.pallas import tpu as pltpu
from jax.sharding import PartitionSpec as P

MESH = pl.DeviceIdType.MESH
epsilon = 1e-05
off_weight = 0.0051
BATCH = 2048
ROWS = 128
WIDE = 1024
EMB = 1536
DP = 16
FEAT = 8
OUT = EMB // DP
TILE = 256
HALF = ROWS // 2
f32 = jnp.float32
bf16 = jnp.bfloat16
NT = (((1,), (1,)), ((), ()))


def column_tiles(body, width=WIDE, tile=TILE):
    @pl.loop(0, width // tile)
    def _(i):
        body(pl.ds(pl.multiple_of(i * tile, tile), tile))


def kernel(
    emb_a, emb_b, w_in, w_out, gain, shift,
    grad_in, grad_gain, grad_shift, diag_loss, row_loss,
    emb, win, wout, gn_sh, inv, hid, act, out, st1, st2, st3, st4, nrm, corr,
    part, far_g, near_gs, near_gr, y_gs, y_gr, gram, go,
    far_s, far_r, near_s, near_r, ys, yr, gact, gh, emb_t,
    core_s, core_r, own_p, far_is, far_ir, near_is, near_ir, y_is, y_ir, gout,
    send_sem, recv_sem, local_sem,
):
    dp, ft = lax.axis_index("dp"), lax.axis_index("feat")
    core, z = lax.rem(dp, 2), lax.rem(dp // 2, 4)
    y_lo, x, y_hi = dp // 8, ft // 2, lax.rem(ft, 2)

    def at_x(step):
        return lax.rem(x + step + 4, 4)

    def at_z(step):
        return lax.rem(z + step + 4, 4)

    def feat_of(step, flip=0):
        return at_x(step) * 2 + (y_hi + flip * (1 - 2 * y_hi))

    def dp_of(step, flip_y=0, flip_core=0):
        yy = y_lo + flip_y * (1 - 2 * y_lo)
        return (yy * 4 + at_z(step)) * 2 + (core + flip_core * (1 - 2 * core))

    x_right, x_left, y_pair = (dp, feat_of(1)), (dp, feat_of(-1)), (dp, feat_of(0, 1))
    z_right, z_left = (dp_of(1), ft), (dp_of(-1), ft)
    y_next, other = (dp_of(0, 1), ft), (dp_of(0, 0, 1), ft)
    peers = [(lax.rem(dp + k, DP), ft) for k in range(1, DP)]

    started = []
    counts = [0, 0]

    def send(src, dst, device):
        i = counts[0]
        counts[0] += 1
        copy = pltpu.make_async_remote_copy(
            src_ref=src, dst_ref=dst, send_sem=send_sem.at[i], recv_sem=recv_sem.at[i],
            device_id=device, device_id_type=MESH,
        )
        copy.start()
        started.append(copy)
        return copy

    def fetch(src, dst):
        i = counts[1]
        counts[1] += 1
        copy = pltpu.make_async_copy(src, dst, local_sem.at[i])
        copy.start()
        return copy

    in_emb = [fetch(emb_a, emb.at[pl.ds(0, ROWS)]), fetch(emb_b, emb.at[pl.ds(ROWS, ROWS)])]
    in_win = fetch(w_in, win)
    in_gs = [fetch(gain, gn_sh.at[pl.ds(0, 1)]), fetch(shift, gn_sh.at[pl.ds(1, 1)])]
    in_wout = fetch(w_out, wout)

    barrier = pltpu.get_barrier_semaphore()
    greeted = peers + [x_right, x_left, y_pair]
    for device in greeted:
        pl.semaphore_signal(barrier, inc=1, device_id=device, device_id_type=MESH)

    def rows(v):
        return pl.ds(v * ROWS, ROWS)

    def share(table):
        return [send(table.at[dp], table.at[dp], device) for device in peers]

    def local_moments(values, table, v, cols):
        center = jnp.sum(values, axis=0, keepdims=True) / ROWS
        spread = jnp.sum((values - center) ** 2, axis=0, keepdims=True)
        table[dp, 0:1, cols] = center
        table[dp, 1:2, cols] = spread

    def global_moments(table, cols):
        centers = table[:, 0, cols]
        center = jnp.sum(centers, axis=0, keepdims=True) / DP
        spread = jnp.sum(table[:, 1, cols], axis=0, keepdims=True) + ROWS * jnp.sum(
            (centers - center) ** 2, axis=0, keepdims=True
        )
        return center, lax.rsqrt(spread / BATCH + epsilon)

    def first_layer():
        for copy in in_emb:
            copy.wait()
        in_win.wait()

        def tile(cols):
            product = jnp.dot(emb[...], win[:, cols], preferred_element_type=f32)
            for v in range(2):
                piece = product[v * ROWS : (v + 1) * ROWS]
                hid[v, :, cols] = piece
                local_moments(piece, st1.at[v], v, cols)

        column_tiles(tile)
        pl.semaphore_wait(barrier, len(greeted))

    def first_norm(v):
        copies = share(st1.at[v])
        yield
        for copy in copies:
            copy.wait_recv()
        if v == 0:
            for copy in in_gs:
                copy.wait()

        def tile(cols):
            center, inverse = global_moments(st1.at[v], cols)
            hat = (hid[v, :, cols] - center) * inverse
            hid[v, :, cols] = hat
            inv[v : v + 1, cols] = inverse
            before = gn_sh[0:1, cols] * hat + gn_sh[1:2, cols]
            act[v, ft, :, cols] = jnp.maximum(before, 0.0).astype(bf16)

        column_tiles(tile)

    def project(v, slot, first=False):
        def tile(cols):
            product = jnp.dot(
                act[v, slot], wout[pl.ds(pl.multiple_of(slot * WIDE, WIDE), WIDE), cols],
                preferred_element_type=f32,
            )
            if first:
                out[v, :, cols] = product
            else:
                out[v, :, cols] += product

        column_tiles(tile)

    def gather_feat(v):
        low, high = pl.ds(0, HALF), pl.ds(HALF, HALF)
        mine, pair = ft, feat_of(0, 1)

        def go_(slot, device, part_rows=None):
            ref = act.at[v, slot] if part_rows is None else act.at[v, slot, part_rows]
            return send(ref, ref, device)

        a = go_(mine, y_pair)
        b = go_(mine, x_right)
        c = go_(mine, x_left)
        if v == 0:
            in_wout.wait()
        project(v, mine, first=True)
        yield
        a.wait_recv()
        d = go_(pair, x_right)
        e = go_(pair, x_left)
        project(v, pair)
        yield
        b.wait_recv()
        f = go_(feat_of(-1), x_right, low)
        c.wait_recv()
        g = go_(feat_of(1), x_left, high)
        project(v, feat_of(-1))
        project(v, feat_of(1))
        yield
        d.wait_recv()
        h = go_(feat_of(-1, 1), x_right, low)
        e.wait_recv()
        i = go_(feat_of(1, 1), x_left, high)
        project(v, feat_of(-1, 1))
        project(v, feat_of(1, 1))
        yield
        f.wait_recv()
        g.wait_recv()
        project(v, feat_of(2))
        yield
        h.wait_recv()
        i.wait_recv()
        project(v, feat_of(2, 1))

    def second_norm(v):
        column_tiles(lambda cols: local_moments(out[v, :, cols], st2.at[v], v, cols))
        copies = share(st2.at[v])
        yield
        for copy in copies:
            copy.wait_recv()

        def tile(cols):
            center, inverse = global_moments(st2.at[v], cols)
            hat = (out[v, :, cols] - center) * inverse
            out[v, :, cols] = hat
            inv[2 + v : 3 + v, cols] = inverse
            nrm[v, dp, :, cols] = hat.astype(bf16)

        column_tiles(tile)

    def inner(v, slot):
        cols = pl.ds(pl.multiple_of(slot * ROWS, ROWS), ROWS)
        part[v, :, cols] = lax.dot_general(
            nrm[v, dp], nrm[v, slot], NT, preferred_element_type=f32
        ).astype(bf16)
        if v == 1:
            corr[pl.ds(slot, 1), :] = jnp.sum(
                nrm[0, slot].astype(f32) * nrm[1, slot].astype(f32), axis=0, keepdims=True
            )

    def gather_dp(v):
        low, high = pl.ds(0, HALF), pl.ds(HALF, HALF)

        def go_(slot, device, part_rows=None):
            ref = nrm.at[v, slot] if part_rows is None else nrm.at[v, slot, part_rows]
            return send(ref, ref, device)

        cores = []

        def have(step, flip):
            slot = dp_of(step, flip)
            cores.append((go_(slot, other), step, flip))
            inner(v, slot)

        def from_core(count):
            for _ in range(count):
                copy, step, flip = cores.pop(0)
                copy.wait_recv()
                inner(v, dp_of(step, flip, 1))

        a = go_(dp, y_next)
        b = go_(dp, z_right)
        c = go_(dp, z_left)
        have(0, 0)
        yield
        a.wait_recv()
        d = go_(dp_of(0, 1), z_right)
        e = go_(dp_of(0, 1), z_left)
        have(0, 1)
        from_core(1)
        yield
        b.wait_recv()
        f = go_(dp_of(-1), z_right, low)
        c.wait_recv()
        g = go_(dp_of(1), z_left, high)
        have(-1, 0)
        have(1, 0)
        from_core(1)
        yield
        d.wait_recv()
        h = go_(dp_of(-1, 1), z_right, low)
        e.wait_recv()
        i = go_(dp_of(1, 1), z_left, high)
        have(-1, 1)
        have(1, 1)
        from_core(2)
        yield
        f.wait_recv()
        g.wait_recv()
        have(2, 0)
        from_core(2)
        yield
        h.wait_recv()
        i.wait_recv()
        have(2, 1)
        from_core(2)

    def sum_gram(v):
        low, high = pl.ds(0, BATCH // 2), pl.ds(BATCH // 2, BATCH // 2)

        def pair_rows(step):
            return pl.ds(pl.multiple_of(at_x(step) * 32, 32), 32)

        far_right = send(part.at[v, pair_rows(2), low], far_g.at[v, 0], x_right)
        far_left = send(part.at[v, pair_rows(2), high], far_g.at[v, 1], x_left)
        near_gs[v, 0] = part[v, pair_rows(1), :]
        near_gs[v, 1] = part[v, pair_rows(-1), :]
        near = [
            send(near_gs.at[v, 0, :, high], near_gr.at[v, 0, :, high], x_right),
            send(near_gs.at[v, 1, :, low], near_gr.at[v, 1, :, low], x_left),
        ]
        yield
        far_right.wait_recv()
        near_gs[v, 0, :, low] = (
            near_gs[v, 0, :, low].astype(f32) + far_g[v, 0].astype(f32)
        ).astype(bf16)
        near.append(send(near_gs.at[v, 0, :, low], near_gr.at[v, 0, :, low], x_right))
        far_left.wait_recv()
        near_gs[v, 1, :, high] = (
            near_gs[v, 1, :, high].astype(f32) + far_g[v, 1].astype(f32)
        ).astype(bf16)
        near.append(send(near_gs.at[v, 1, :, high], near_gr.at[v, 1, :, high], x_left))
        yield
        for copy in near:
            copy.wait_recv()

        def line_sum(flip):
            h = y_hi + flip * (1 - 2 * y_hi)
            block = pl.ds(pl.multiple_of(h * 16, 16), 16)
            return (
                part[v, pl.ds(pl.multiple_of(feat_of(0, flip) * 16, 16), 16), :].astype(f32)
                + near_gr[v, 0, block, :].astype(f32)
                + near_gr[v, 1, block, :].astype(f32)
            )

        y_gs[v] = line_sum(1).astype(bf16)
        a = send(y_gs.at[v], y_gr.at[v], y_pair)
        yield
        a.wait_recv()

        def slot(step, flip=0):
            return pl.ds(pl.multiple_of(feat_of(step, flip) * 16, 16), 16)

        gram[v, slot(0), :] = (line_sum(0) + y_gr[v].astype(f32)).astype(bf16)

        def go_(block, device, cols=None):
            ref = gram.at[v, block] if cols is None else gram.at[v, block, cols]
            return send(ref, ref, device)

        a = go_(slot(0), y_pair)
        b = go_(slot(0), x_right)
        c = go_(slot(0), x_left)
        yield
        a.wait_recv()
        d = go_(slot(0, 1), x_right)
        e = go_(slot(0, 1), x_left)
        b.wait_recv()
        f = go_(slot(-1), x_right, low)
        c.wait_recv()
        g = go_(slot(1), x_left, high)
        yield
        d.wait_recv()
        h = go_(slot(-1, 1), x_right, low)
        e.wait_recv()
        i = go_(slot(1, 1), x_left, high)
        yield
        for copy in (f, g, h, i):
            copy.wait_recv()

    factor = BATCH / 64.0
    coeff = 2.0 * off_weight / (BATCH * BATCH)

    def losses():
        diag = jnp.sum(corr[...], axis=0, keepdims=True) / BATCH
        diag_loss[...] = (1.0 - diag) ** 2 - off_weight * diag**2
        corr[0:1, :] = -2.0 * (1.0 - diag) - 2.0 * off_weight * diag

    def row_losses():
        total = jnp.zeros((ROWS, ROWS), f32)
        for k in range(BATCH // ROWS):
            cols = slice(k * ROWS, (k + 1) * ROWS)
            total += gram[0, :, cols].astype(f32) * gram[1, :, cols].astype(f32)
        total = jnp.sum(total.T, axis=0, keepdims=True)
        row_loss[...] = total / (BATCH * WIDE * FEAT)

    def output_back(v):
        def tile(cols):
            product = jnp.dot(
                gram[1 - v], nrm[v, :, :, cols].reshape(BATCH, TILE), preferred_element_type=f32
            )
            upstream = factor * (
                coeff * product + nrm[1 - v, dp, :, cols].astype(f32) * corr[0:1, cols] / BATCH
            )
            gact[v, :, cols] = upstream
            st3[v, dp, 0:1, cols] = jnp.sum(upstream, axis=0, keepdims=True)
            st3[v, dp, 1:2, cols] = jnp.sum(upstream * out[v, :, cols], axis=0, keepdims=True)

        column_tiles(tile)
        copies = share(st3.at[v])
        yield
        for copy in copies:
            copy.wait_recv()

        def finish(cols):
            up = jnp.sum(st3[v, :, 0, cols], axis=0, keepdims=True) / BATCH
            dot = jnp.sum(st3[v, :, 1, cols], axis=0, keepdims=True) / BATCH
            go[v, :, cols] = (
                inv[2 + v : 3 + v, cols] * (gact[v, :, cols] - up - out[v, :, cols] * dot)
            ).astype(bf16)

        column_tiles(finish)

    def active_back(v):
        def block(step, flip, store):
            first = feat_of(step, flip) * WIDE

            def tile(cols):
                store(
                    cols,
                    lax.dot_general(
                        go[v], wout[pl.ds(pl.multiple_of(first + cols.start, TILE), TILE), :], NT,
                        preferred_element_type=f32,
                    ),
                )

            column_tiles(tile)

        low, high = pl.ds(0, HALF), pl.ds(HALF, HALF)

        def keep(ref):
            def store(cols, value):
                ref[:, cols] = value.astype(bf16)

            return store

        def far(flip):
            block(2, flip, keep(far_s.at[v, flip]))
            return [
                send(far_s.at[v, flip, low], far_r.at[v, flip, 0], x_right),
                send(far_s.at[v, flip, high], far_r.at[v, flip, 1], x_left),
            ]

        def near(flip):
            block(1, flip, keep(near_s.at[v, flip, 0]))
            a = send(near_s.at[v, flip, 0, high], near_r.at[v, flip, 0, high], x_right)
            block(-1, flip, keep(near_s.at[v, flip, 1]))
            b = send(near_s.at[v, flip, 1, low], near_r.at[v, flip, 1, low], x_left)
            return [a, b]

        def relay(flip, fars, nears):
            for side, half, device in ((0, low, x_right), (1, high, x_left)):
                fars[side].wait_recv()
                near_s[v, flip, side, half] = (
                    near_s[v, flip, side, half].astype(f32) + far_r[v, flip, side].astype(f32)
                ).astype(bf16)
                nears.append(
                    send(near_s.at[v, flip, side, half], near_r.at[v, flip, side, half], device)
                )

        fars1 = far(1)
        nears1 = near(1)
        yield
        fars0 = far(0)
        relay(1, fars1, nears1)
        nears0 = near(0)
        yield

        def store_own(cols, value):
            gact[v, :, cols] = value

        block(0, 1, store_own)
        for copy in nears1:
            copy.wait_recv()
        ys[v] = (
            gact[v] + near_r[v, 1, 0].astype(f32) + near_r[v, 1, 1].astype(f32)
        ).astype(bf16)
        last = send(ys.at[v], yr.at[v], y_pair)
        yield
        relay(0, fars0, nears0)
        block(0, 0, store_own)
        yield
        for copy in nears0 + [last]:
            copy.wait_recv()

    def first_back(v):
        def tile(cols):
            hat = hid[v, :, cols]
            grad = (
                gact[v, :, cols]
                + near_r[v, 0, 0, :, cols].astype(f32)
                + near_r[v, 0, 1, :, cols].astype(f32)
                + yr[v, :, cols].astype(f32)
            )
            before = gn_sh[0:1, cols] * hat + gn_sh[1:2, cols]
            grad = jnp.where(before > 0, grad, 0.0)
            gact[v, :, cols] = grad
            st4[v, dp, 0:1, cols] = jnp.sum(grad, axis=0, keepdims=True)
            st4[v, dp, 1:2, cols] = jnp.sum(grad * hat, axis=0, keepdims=True)

        column_tiles(tile)
        copies = share(st4.at[v])
        yield
        for copy in copies:
            copy.wait_recv()

        def finish(cols):
            up = jnp.sum(st4[v, :, 0, cols], axis=0, keepdims=True)
            dot = jnp.sum(st4[v, :, 1, cols], axis=0, keepdims=True)
            gh[rows(v), cols] = (
                gn_sh[0:1, cols] * inv[v : v + 1, cols]
                * (gact[v, :, cols] - up / BATCH - hid[v, :, cols] * (dot / BATCH))
            ).astype(bf16)
            if v == 0:
                grad_shift[:, cols] = up
                grad_gain[:, cols] = dot
            else:
                grad_shift[:, cols] += up
                grad_gain[:, cols] += dot

        column_tiles(finish)

    def transpose_emb():
        for k in range(EMB // ROWS):
            cols = slice(k * ROWS, (k + 1) * ROWS)
            emb_t[cols, :] = emb[:, cols].T

    def last_layer():
        low, high = pl.ds(0, OUT // 2), pl.ds(OUT // 2, OUT // 2)

        def partial(step, flip_y, flip_core, store):
            target = dp_of(step, flip_y, flip_core)
            left = emb_t[pl.ds(pl.multiple_of(target * OUT, OUT), OUT), :]
            column_tiles(
                lambda cols: store(
                    cols, jnp.dot(left, gh[:, cols], preferred_element_type=f32)
                )
            )

        order = [(2, 1), (1, 1), (-1, 1), (2, 0), (1, 0), (-1, 0), (0, 1), (0, 0)]
        crossing = {}
        for n, (step, flip) in enumerate(order):
            def store(cols, value, n=n):
                core_s[n, :, cols] = value.astype(bf16)

            partial(step, flip, 1, store)
            crossing[step, flip] = send(core_s.at[n], core_r.at[n], other)

        def chip_sum(step, flip, keep):
            n = order.index((step, flip))

            def store(cols, value):
                own_p[n, :, cols] = value

            partial(step, flip, 0, store)
            crossing[step, flip].wait_recv()

            def tile(cols):
                keep(cols, own_p[n, :, cols] + core_r[n, :, cols].astype(f32))

            column_tiles(tile)

        def keep(ref):
            def store(cols, value):
                ref[:, cols] = value.astype(bf16)

            return store

        def far(flip):
            chip_sum(2, flip, keep(far_is.at[flip]))
            return [
                send(far_is.at[flip, low], far_ir.at[flip, 0], z_right),
                send(far_is.at[flip, high], far_ir.at[flip, 1], z_left),
            ]

        def near(flip):
            chip_sum(1, flip, keep(near_is.at[flip, 0]))
            a = send(near_is.at[flip, 0, high], near_ir.at[flip, 0, high], z_right)
            chip_sum(-1, flip, keep(near_is.at[flip, 1]))
            b = send(near_is.at[flip, 1, low], near_ir.at[flip, 1, low], z_left)
            return [a, b]

        def relay(flip, fars, nears):
            for side, half, device in ((0, low, z_right), (1, high, z_left)):
                fars[side].wait_recv()
                near_is[flip, side, half] = (
                    near_is[flip, side, half].astype(f32) + far_ir[flip, side].astype(f32)
                ).astype(bf16)
                nears.append(
                    send(near_is.at[flip, side, half], near_ir.at[flip, side, half], device)
                )

        def line_sum(flip, store):
            n = order.index((0, flip))

            def tile(cols):
                store(
                    cols,
                    own_p[n, :, cols]
                    + near_ir[flip, 0, :, cols].astype(f32)
                    + near_ir[flip, 1, :, cols].astype(f32),
                )

            column_tiles(tile)

        fars1 = far(1)
        nears1 = near(1)
        fars0 = far(0)
        relay(1, fars1, nears1)
        nears0 = near(0)

        def own(flip):
            n = order.index((0, flip))

            def store(cols, value):
                own_p[n, :, cols] = value

            chip_sum(0, flip, store)

        own(1)
        for copy in nears1:
            copy.wait_recv()
        line_sum(1, keep(y_is))
        last = send(y_is, y_ir, y_next)
        relay(0, fars0, nears0)
        own(0)
        for copy in nears0 + [last]:
            copy.wait_recv()

        def finish(cols, value):
            gout[:, cols] = value + y_ir[:, cols].astype(f32)

        line_sum(0, finish)
        store_out = fetch(gout, grad_in)
        store_out.wait()

    def together(*stages):
        stages = list(stages)
        while stages:
            for stage in list(stages):
                if next(stage, True):
                    stages.remove(stage)

    both = lambda stage: together(stage(0), stage(1))
    first_layer()
    both(first_norm)
    transpose_emb()
    both(gather_feat)
    both(second_norm)
    both(gather_dp)
    losses()
    both(sum_gram)
    both(output_back)
    row_losses()
    both(active_back)
    both(first_back)
    last_layer()
    for copy in started:
        copy.wait_send()


def scratch():
    v = pltpu.VMEM
    return [
        v((2 * ROWS, EMB), bf16), v((EMB, WIDE), bf16), v((FEAT * WIDE, WIDE), bf16),
        v((2, WIDE), f32), v((4, WIDE), f32), v((2, ROWS, WIDE), f32), v((2, FEAT, ROWS, WIDE), bf16),
        v((2, ROWS, WIDE), f32),
        v((2, DP, 2, WIDE), f32), v((2, DP, 2, WIDE), f32),
        v((2, DP, 2, WIDE), f32), v((2, DP, 2, WIDE), f32),
        v((2, DP, ROWS, WIDE), bf16), v((DP, WIDE), f32),
        v((2, ROWS, BATCH), bf16), v((2, 2, 32, BATCH // 2), bf16),
        v((2, 2, 32, BATCH), bf16), v((2, 2, 32, BATCH), bf16),
        v((2, 16, BATCH), bf16), v((2, 16, BATCH), bf16), v((2, ROWS, BATCH), bf16),
        v((2, ROWS, WIDE), bf16),
        v((2, 2, ROWS, WIDE), bf16), v((2, 2, 2, HALF, WIDE), bf16),
        v((2, 2, 2, ROWS, WIDE), bf16), v((2, 2, 2, ROWS, WIDE), bf16),
        v((2, ROWS, WIDE), bf16), v((2, ROWS, WIDE), bf16), v((2, ROWS, WIDE), f32),
        v((2 * ROWS, WIDE), bf16), v((EMB, 2 * ROWS), bf16),
        v((8, OUT, WIDE), bf16), v((8, OUT, WIDE), bf16), v((8, OUT, WIDE), f32),
        v((2, OUT, WIDE), bf16), v((2, 2, OUT // 2, WIDE), bf16),
        v((2, 2, OUT, WIDE), bf16), v((2, 2, OUT, WIDE), bf16),
        v((OUT, WIDE), bf16), v((OUT, WIDE), bf16), v((OUT, WIDE), f32),
        pltpu.SemaphoreType.DMA((260,)), pltpu.SemaphoreType.DMA((260,)),
        pltpu.SemaphoreType.DMA((8,)),
    ]


def shards(emb_a, emb_b, w_in, w_out, gain, shift):
    anywhere = pl.BlockSpec(memory_space=pl.ANY)
    near = pl.BlockSpec(memory_space=pltpu.VMEM)
    results = pl.pallas_call(
        kernel,
        out_shape=(
            jax.ShapeDtypeStruct((OUT, WIDE), f32),
            jax.ShapeDtypeStruct((1, WIDE), f32),
            jax.ShapeDtypeStruct((1, WIDE), f32),
            jax.ShapeDtypeStruct((1, WIDE), f32),
            jax.ShapeDtypeStruct((1, ROWS), f32),
        ),
        in_specs=[anywhere] * 6,
        out_specs=(anywhere, near, near, near, near),
        scratch_shapes=scratch(),
        compiler_params=pltpu.CompilerParams(
            collective_id=0, has_side_effects=True, vmem_limit_bytes=62 * 2**20
        ),
        cost_estimate=pl.CostEstimate(flops=14 * 10**9, bytes_accessed=24 * 2**20, transcendentals=0),
    )(emb_a, emb_b, w_in, w_out, gain.reshape(1, WIDE), shift.reshape(1, WIDE))
    return (results[0],) + tuple(r.reshape(-1) for r in results[1:])


def solution(mesh):
    return jax.shard_map(
        shards,
        mesh=mesh,
        in_specs=(
            P("dp", None), P("dp", None), P(None, "feat"), P(None, "feat"), P("feat"), P("feat"),
        ),
        out_specs=(P("dp", "feat"), P("feat"), P("feat"), P("feat"), P("dp")),
        check_vma=False,
    )
```

```python
import functools
import math

import jax
import jax.numpy as jnp
from jax import lax
from jax.experimental import pallas as pl
from jax.experimental.pallas import tpu as pltpu
from jax.sharding import PartitionSpec as P

MESH = pl.DeviceIdType.MESH
epsilon = 1e-05
off_weight = 0.0051
BATCH = 2048
ROWS = 128
WIDE = 1024
EMB = 1536
DP = 16
FEAT = 8
OUT = EMB // DP
TILE = 256
PIECE = WIDE // 2
HALF = ROWS // 2
f32 = jnp.float32
bf16 = jnp.bfloat16
NT = (((1,), (1,)), ((), ()))


def column_tiles(body, width=WIDE, tile=TILE):
    @pl.loop(0, width // tile)
    def _(i):
        body(pl.ds(pl.multiple_of(i * tile, tile), tile))


def kernel(
    emb_a, emb_b, w_in, w_out, gain, shift,
    grad_in, grad_gain, grad_shift, diag_loss, row_loss,
    emb, win, wout, gn_sh, inv, hid, act, out, st1, st2, st3, st4, nrm, corr,
    part, far_g, near_gs, near_gr, y_gs, y_gr, gram, go,
    far_s, far_r, near_s, near_r, ys, yr, gact, gh, emb_t,
    core_r, far_is, far_ir, near_is, near_ir, y_is, y_ir, gout,
    send_sem, recv_sem, local_sem,
):
    dp, ft = lax.axis_index("dp"), lax.axis_index("feat")
    core, z = lax.rem(dp, 2), lax.rem(dp // 2, 4)
    y_lo, x, y_hi = dp // 8, ft // 2, lax.rem(ft, 2)

    def at_x(step):
        return lax.rem(x + step + 4, 4)

    def at_z(step):
        return lax.rem(z + step + 4, 4)

    def feat_of(step, flip=0):
        return at_x(step) * 2 + (y_hi + flip * (1 - 2 * y_hi))

    def dp_of(step, flip_y=0, flip_core=0):
        yy = y_lo + flip_y * (1 - 2 * y_lo)
        return (yy * 4 + at_z(step)) * 2 + (core + flip_core * (1 - 2 * core))

    x_right, x_left, y_pair = (dp, feat_of(1)), (dp, feat_of(-1)), (dp, feat_of(0, 1))
    z_right, z_left = (dp_of(1), ft), (dp_of(-1), ft)
    y_next, other = (dp_of(0, 1), ft), (dp_of(0, 0, 1), ft)
    peers = [(lax.rem(dp + k, DP), ft) for k in range(1, DP)]

    waiting = []
    counts = [0, 0, 0]

    def size(ref):
        return math.prod(ref.shape) * jnp.dtype(ref.dtype).itemsize

    def all_of(sem, total):
        count = total // (16 * 2 * WIDE)
        ref = wout.at[pl.ds(0, 16 * count)]
        return pltpu.make_async_copy(ref, ref, sem)

    class Sender:
        def __init__(self):
            self.sem = send_sem.at[counts[2]]
            counts[2] += 1
            self.total = 0
            senders.append(self)

        def __call__(self, src, dst, device):
            i = counts[0]
            counts[0] += 1
            copy = pltpu.make_async_remote_copy(
                src_ref=src, dst_ref=dst, send_sem=self.sem, recv_sem=recv_sem.at[i],
                device_id=device, device_id_type=MESH,
            )
            copy.start()
            self.total += size(src)
            return copy

        def finish(self):
            all_of(self.sem, self.total).wait()

    senders = []

    class Share:
        def __init__(self, table):
            self.leave, self.land = send_sem.at[counts[2]], recv_sem.at[counts[0]]
            counts[2] += 1
            counts[0] += 1
            for device in peers:
                pltpu.make_async_remote_copy(
                    src_ref=table.at[dp], dst_ref=table.at[dp], send_sem=self.leave,
                    recv_sem=self.land, device_id=device, device_id_type=MESH,
                ).start()
            self.others = table.at[pl.ds(0, DP - 1)]
            senders.append(self)

        def wait_recv(self):
            pltpu.make_async_copy(self.others, self.others, self.land).wait()

        def finish(self):
            pltpu.make_async_copy(self.others, self.others, self.leave).wait()

    def fetch(src, dst):
        i = counts[1]
        counts[1] += 1
        copy = pltpu.make_async_copy(src, dst, local_sem.at[i])
        copy.start()
        return copy

    in_emb = [fetch(emb_a, emb.at[pl.ds(0, ROWS)]), fetch(emb_b, emb.at[pl.ds(ROWS, ROWS)])]
    in_win = fetch(w_in, win)
    in_gs = [fetch(gain, gn_sh.at[pl.ds(0, 1)]), fetch(shift, gn_sh.at[pl.ds(1, 1)])]

    barrier = pltpu.get_barrier_semaphore()
    greeted = peers + [x_right, x_left, y_pair]
    for device in greeted:
        pl.semaphore_signal(barrier, inc=1, device_id=device, device_id_type=MESH)

    def rows(v):
        return pl.ds(v * ROWS, ROWS)

    def local_moments(values, table, row, cols):
        center = jnp.sum(values, axis=0, keepdims=True) / ROWS
        spread = jnp.sum((values - center) ** 2, axis=0, keepdims=True)
        table[dp, row : row + 1, cols] = center
        table[dp, row + 1 : row + 2, cols] = spread

    def global_moments(table, row, cols):
        centers = table[:, row, cols]
        center = jnp.sum(centers, axis=0, keepdims=True) / DP
        spread = jnp.sum(table[:, row + 1, cols], axis=0, keepdims=True) + ROWS * jnp.sum(
            (centers - center) ** 2, axis=0, keepdims=True
        )
        return center, lax.rsqrt(spread / BATCH + epsilon)

    def first_layer():
        for copy in in_emb:
            copy.wait()
        in_win.wait()
        waiting.append(fetch(w_out, wout))

        def tile(cols):
            product = jnp.dot(emb[...], win[:, cols], preferred_element_type=f32)
            for v in range(2):
                piece = product[v * ROWS : (v + 1) * ROWS]
                hid[v, :, cols] = piece
                local_moments(piece, st1, 2 * v, cols)

        column_tiles(tile)
        pl.semaphore_wait(barrier, len(greeted))

    def first_norm(v):
        if v == 0:
            exchange = Share(st1)
            yield
            exchange.wait_recv()
            for copy in in_gs:
                copy.wait()

        def tile(cols):
            center, inverse = global_moments(st1, 2 * v, cols)
            hat = (hid[v, :, cols] - center) * inverse
            hid[v, :, cols] = hat
            inv[v : v + 1, cols] = inverse
            before = gn_sh[0:1, cols] * hat + gn_sh[1:2, cols]
            act[v, ft, :, cols] = jnp.maximum(before, 0.0).astype(bf16)

        column_tiles(tile)
        yield

    def project(v, slot, first=False):
        def tile(cols):
            product = jnp.dot(
                act[v, slot], wout[pl.ds(pl.multiple_of(slot * WIDE, WIDE), WIDE), cols],
                preferred_element_type=f32,
            )
            if first:
                out[v, :, cols] = product
            else:
                out[v, :, cols] += product

        column_tiles(tile)

    def gather_feat(v):
        send = Sender()
        low, high = pl.ds(0, HALF), pl.ds(HALF, HALF)
        mine, pair = ft, feat_of(0, 1)

        def go_(slot, device, part_rows=None):
            ref = act.at[v, slot] if part_rows is None else act.at[v, slot, part_rows]
            return send(ref, ref, device)

        a = go_(mine, y_pair)
        b = go_(mine, x_right)
        c = go_(mine, x_left)
        if v == 0:
            waiting.pop().wait()
        project(v, mine, first=True)
        yield
        a.wait_recv()
        d = go_(pair, x_right)
        e = go_(pair, x_left)
        project(v, pair)
        yield
        b.wait_recv()
        f = go_(feat_of(-1), x_right, low)
        c.wait_recv()
        g = go_(feat_of(1), x_left, high)
        project(v, feat_of(-1))
        project(v, feat_of(1))
        yield
        d.wait_recv()
        h = go_(feat_of(-1, 1), x_right, low)
        e.wait_recv()
        i = go_(feat_of(1, 1), x_left, high)
        project(v, feat_of(-1, 1))
        project(v, feat_of(1, 1))
        yield
        f.wait_recv()
        g.wait_recv()
        project(v, feat_of(2))
        yield
        h.wait_recv()
        i.wait_recv()
        project(v, feat_of(2, 1))

    def second_norm(v):
        column_tiles(lambda cols: local_moments(out[v, :, cols], st2.at[v], 0, cols))
        exchange = Share(st2.at[v])
        yield
        exchange.wait_recv()

        def tile(cols):
            center, inverse = global_moments(st2.at[v], 0, cols)
            hat = (out[v, :, cols] - center) * inverse
            out[v, :, cols] = hat
            inv[2 + v : 3 + v, cols] = inverse
            nrm[v, dp, :, cols] = hat.astype(bf16)

        column_tiles(tile)

    def inner(v, slot):
        cols = pl.ds(pl.multiple_of(slot * ROWS, ROWS), ROWS)
        part[v, :, cols] = lax.dot_general(
            nrm[v, dp], nrm[v, slot], NT, preferred_element_type=f32
        ).astype(bf16)
        if v == 1:
            corr[pl.ds(slot, 1), :] = jnp.sum(
                nrm[0, slot].astype(f32) * nrm[1, slot].astype(f32), axis=0, keepdims=True
            )

    def gather_dp(v):
        send = Sender()
        low, high = pl.ds(0, HALF), pl.ds(HALF, HALF)

        def go_(slot, device, part_rows=None):
            ref = nrm.at[v, slot] if part_rows is None else nrm.at[v, slot, part_rows]
            return send(ref, ref, device)

        cores = []

        def have(step, flip):
            slot = dp_of(step, flip)
            cores.append((go_(slot, other), step, flip))
            inner(v, slot)

        def from_core(count):
            for _ in range(count):
                copy, step, flip = cores.pop(0)
                copy.wait_recv()
                inner(v, dp_of(step, flip, 1))

        a = go_(dp, y_next)
        b = go_(dp, z_right)
        c = go_(dp, z_left)
        have(0, 0)
        yield
        a.wait_recv()
        d = go_(dp_of(0, 1), z_right)
        e = go_(dp_of(0, 1), z_left)
        have(0, 1)
        from_core(1)
        yield
        b.wait_recv()
        f = go_(dp_of(-1), z_right, low)
        c.wait_recv()
        g = go_(dp_of(1), z_left, high)
        have(-1, 0)
        have(1, 0)
        from_core(1)
        yield
        d.wait_recv()
        h = go_(dp_of(-1, 1), z_right, low)
        e.wait_recv()
        i = go_(dp_of(1, 1), z_left, high)
        have(-1, 1)
        have(1, 1)
        from_core(2)
        yield
        f.wait_recv()
        g.wait_recv()
        have(2, 0)
        from_core(2)
        yield
        h.wait_recv()
        i.wait_recv()
        have(2, 1)
        from_core(2)

    def sum_gram(v):
        send = Sender()
        low, high = pl.ds(0, BATCH // 2), pl.ds(BATCH // 2, BATCH // 2)

        def pair_rows(step):
            return pl.ds(pl.multiple_of(at_x(step) * 32, 32), 32)

        far_right = send(part.at[v, pair_rows(2), low], far_g.at[v, 0], x_right)
        far_left = send(part.at[v, pair_rows(2), high], far_g.at[v, 1], x_left)
        near_gs[v, 0] = part[v, pair_rows(1), :]
        near_gs[v, 1] = part[v, pair_rows(-1), :]
        near = [
            send(near_gs.at[v, 0, :, high], near_gr.at[v, 0, :, high], x_right),
            send(near_gs.at[v, 1, :, low], near_gr.at[v, 1, :, low], x_left),
        ]
        yield
        far_right.wait_recv()
        near_gs[v, 0, :, low] = (
            near_gs[v, 0, :, low].astype(f32) + far_g[v, 0].astype(f32)
        ).astype(bf16)
        near.append(send(near_gs.at[v, 0, :, low], near_gr.at[v, 0, :, low], x_right))
        far_left.wait_recv()
        near_gs[v, 1, :, high] = (
            near_gs[v, 1, :, high].astype(f32) + far_g[v, 1].astype(f32)
        ).astype(bf16)
        near.append(send(near_gs.at[v, 1, :, high], near_gr.at[v, 1, :, high], x_left))
        yield
        for copy in near:
            copy.wait_recv()

        def line_sum(flip):
            h = y_hi + flip * (1 - 2 * y_hi)
            block = pl.ds(pl.multiple_of(h * 16, 16), 16)
            return (
                part[v, pl.ds(pl.multiple_of(feat_of(0, flip) * 16, 16), 16), :].astype(f32)
                + near_gr[v, 0, block, :].astype(f32)
                + near_gr[v, 1, block, :].astype(f32)
            )

        y_gs[v] = line_sum(1).astype(bf16)
        a = send(y_gs.at[v], y_gr.at[v], y_pair)
        yield
        a.wait_recv()

        def slot(step, flip=0):
            return pl.ds(pl.multiple_of(feat_of(step, flip) * 16, 16), 16)

        gram[v, slot(0), :] = (line_sum(0) + y_gr[v].astype(f32)).astype(bf16)

        def go_(block, device, cols=None):
            ref = gram.at[v, block] if cols is None else gram.at[v, block, cols]
            return send(ref, ref, device)

        a = go_(slot(0), y_pair)
        b = go_(slot(0), x_right)
        c = go_(slot(0), x_left)
        yield
        a.wait_recv()
        d = go_(slot(0, 1), x_right)
        e = go_(slot(0, 1), x_left)
        b.wait_recv()
        f = go_(slot(-1), x_right, low)
        c.wait_recv()
        g = go_(slot(1), x_left, high)
        yield
        d.wait_recv()
        h = go_(slot(-1, 1), x_right, low)
        e.wait_recv()
        i = go_(slot(1, 1), x_left, high)
        yield
        for copy in (f, g, h, i):
            copy.wait_recv()

    factor = BATCH / 64.0
    coeff = 2.0 * off_weight / (BATCH * BATCH)

    def losses():
        diag = jnp.sum(corr[...], axis=0, keepdims=True) / BATCH
        diag_loss[...] = (1.0 - diag) ** 2 - off_weight * diag**2
        corr[0:1, :] = -2.0 * (1.0 - diag) - 2.0 * off_weight * diag

    def row_losses():
        total = jnp.zeros((ROWS, ROWS), f32)
        for k in range(BATCH // ROWS):
            cols = slice(k * ROWS, (k + 1) * ROWS)
            total += gram[0, :, cols].astype(f32) * gram[1, :, cols].astype(f32)
        total = jnp.sum(total.T, axis=0, keepdims=True)
        row_loss[...] = total / (BATCH * WIDE * FEAT)

    def output_back(v):
        def tile(cols):
            product = jnp.dot(
                gram[1 - v], nrm[v, :, :, cols].reshape(BATCH, TILE), preferred_element_type=f32
            )
            upstream = factor * (
                coeff * product + nrm[1 - v, dp, :, cols].astype(f32) * corr[0:1, cols] / BATCH
            )
            gact[v, :, cols] = upstream
            st3[v, dp, 0:1, cols] = jnp.sum(upstream, axis=0, keepdims=True)
            st3[v, dp, 1:2, cols] = jnp.sum(upstream * out[v, :, cols], axis=0, keepdims=True)

        column_tiles(tile)
        exchange = Share(st3.at[v])
        yield
        exchange.wait_recv()

        def finish(cols):
            up = jnp.sum(st3[v, :, 0, cols], axis=0, keepdims=True) / BATCH
            dot = jnp.sum(st3[v, :, 1, cols], axis=0, keepdims=True) / BATCH
            go[v, :, cols] = (
                inv[2 + v : 3 + v, cols] * (gact[v, :, cols] - up - out[v, :, cols] * dot)
            ).astype(bf16)

        column_tiles(finish)

    def keep(ref):
        def store(cols, value):
            ref[:, cols] = value.astype(bf16)

        return store

    stores = []

    def active_back(v, h):
        send = Sender()
        def block(step, flip, store):
            first = feat_of(step, flip) * WIDE + h * PIECE

            def tile(cols):
                store(
                    cols,
                    lax.dot_general(
                        go[v], wout[pl.ds(pl.multiple_of(first + cols.start, TILE), TILE), :], NT,
                        preferred_element_type=f32,
                    ),
                )

            column_tiles(tile, PIECE)

        low, high = pl.ds(0, HALF), pl.ds(HALF, HALF)

        def far(flip):
            block(2, flip, keep(far_s.at[v, h, flip]))
            return [
                send(far_s.at[v, h, flip, low], far_r.at[v, h, flip, 0], x_right),
                send(far_s.at[v, h, flip, high], far_r.at[v, h, flip, 1], x_left),
            ]

        def near(flip):
            block(1, flip, keep(near_s.at[v, h, flip, 0]))
            a = send(near_s.at[v, h, flip, 0, high], near_r.at[v, h, flip, 0, high], x_right)
            block(-1, flip, keep(near_s.at[v, h, flip, 1]))
            b = send(near_s.at[v, h, flip, 1, low], near_r.at[v, h, flip, 1, low], x_left)
            return [a, b]

        def relay(flip, fars, nears):
            for side, half, device in ((0, low, x_right), (1, high, x_left)):
                fars[side].wait_recv()
                near_s[v, h, flip, side, half] = (
                    near_s[v, h, flip, side, half].astype(f32)
                    + far_r[v, h, flip, side].astype(f32)
                ).astype(bf16)
                nears.append(
                    send(
                        near_s.at[v, h, flip, side, half], near_r.at[v, h, flip, side, half], device
                    )
                )

        fars1 = far(1)
        nears1 = near(1)
        yield
        fars0 = far(0)
        relay(1, fars1, nears1)
        nears0 = near(0)
        yield
        mine = pl.ds(h * PIECE, PIECE)

        def store_own(cols, value):
            gact[v, :, pl.ds(pl.multiple_of(h * PIECE + cols.start, TILE), TILE)] = value

        block(0, 1, store_own)
        for copy in nears1:
            copy.wait_recv()
        ys[v, h] = (
            gact[v, :, mine] + near_r[v, h, 1, 0].astype(f32) + near_r[v, h, 1, 1].astype(f32)
        ).astype(bf16)
        last = send(ys.at[v, h], yr.at[v, h], y_pair)
        yield
        relay(0, fars0, nears0)
        block(0, 0, store_own)
        yield
        for copy in nears0 + [last]:
            copy.wait_recv()

    def first_back(h):
        def tile(v, cols):
            full = pl.ds(pl.multiple_of(h * PIECE + cols.start, TILE), TILE)
            hat = hid[v, :, full]
            grad = (
                gact[v, :, full]
                + near_r[v, h, 0, 0, :, cols].astype(f32)
                + near_r[v, h, 0, 1, :, cols].astype(f32)
                + yr[v, h, :, cols].astype(f32)
            )
            before = gn_sh[0:1, full] * hat + gn_sh[1:2, full]
            grad = jnp.where(before > 0, grad, 0.0)
            gact[v, :, full] = grad
            st4[h, dp, 2 * v : 2 * v + 1, cols] = jnp.sum(grad, axis=0, keepdims=True)
            st4[h, dp, 2 * v + 1 : 2 * v + 2, cols] = jnp.sum(grad * hat, axis=0, keepdims=True)

        column_tiles(functools.partial(tile, 1), PIECE)
        yield
        column_tiles(functools.partial(tile, 0), PIECE)
        exchange = Share(st4.at[h])
        yield
        exchange.wait_recv()

        def finish(cols):
            full = pl.ds(pl.multiple_of(h * PIECE + cols.start, TILE), TILE)
            sums = [jnp.sum(st4[h, :, k, cols], axis=0, keepdims=True) for k in range(4)]
            for v in range(2):
                up, dot = sums[2 * v], sums[2 * v + 1]
                gh[rows(v), full] = (
                    gn_sh[0:1, full] * inv[v : v + 1, full]
                    * (gact[v, :, full] - up / BATCH - hid[v, :, full] * (dot / BATCH))
                ).astype(bf16)
            grad_shift[:, full] = sums[0] + sums[2]
            grad_gain[:, full] = sums[1] + sums[3]

        column_tiles(finish, PIECE)

    def transpose_emb():
        for k in range(EMB // ROWS):
            cols = slice(k * ROWS, (k + 1) * ROWS)
            emb_t[cols, :] = emb[:, cols].T

    def last_layer(h):
        send = Sender()
        low, high = pl.ds(0, OUT // 2), pl.ds(OUT // 2, OUT // 2)
        mine = pl.ds(h * PIECE, PIECE)

        def product(cols):
            full = pl.ds(pl.multiple_of(h * PIECE + cols.start, TILE), TILE)
            win[:, full] = jnp.dot(
                emb_t[...], gh[:, full], preferred_element_type=f32
            ).astype(bf16)

        def block(step, flip_y, flip_core):
            target = dp_of(step, flip_y, flip_core)
            return win.at[pl.ds(pl.multiple_of(target * OUT, OUT), OUT), mine]

        column_tiles(product, PIECE)
        order = [(2, 1), (1, 1), (-1, 1), (2, 0), (1, 0), (-1, 0), (0, 1), (0, 0)]
        crossing = {}
        for n, (step, flip) in enumerate(order):
            crossing[step, flip] = send(block(step, flip, 1), core_r.at[h, n], other)
        yield

        def chip_sum(step, flip):
            n = order.index((step, flip))
            crossing[step, flip].wait_recv()
            return block(step, flip, 0)[...].astype(f32) + core_r[h, n].astype(f32)

        def far(flip):
            far_is[h, flip] = chip_sum(2, flip).astype(bf16)
            return [
                send(far_is.at[h, flip, low], far_ir.at[h, flip, 0], z_right),
                send(far_is.at[h, flip, high], far_ir.at[h, flip, 1], z_left),
            ]

        def near(flip):
            near_is[h, flip, 0] = chip_sum(1, flip).astype(bf16)
            a = send(near_is.at[h, flip, 0, high], near_ir.at[h, flip, 0, high], z_right)
            near_is[h, flip, 1] = chip_sum(-1, flip).astype(bf16)
            b = send(near_is.at[h, flip, 1, low], near_ir.at[h, flip, 1, low], z_left)
            return [a, b]

        def relay(flip, fars, nears):
            for side, half, device in ((0, low, z_right), (1, high, z_left)):
                fars[side].wait_recv()
                near_is[h, flip, side, half] = (
                    near_is[h, flip, side, half].astype(f32) + far_ir[h, flip, side].astype(f32)
                ).astype(bf16)
                nears.append(
                    send(near_is.at[h, flip, side, half], near_ir.at[h, flip, side, half], device)
                )

        def line_sum(flip):
            return (
                chip_sum(0, flip)
                + near_ir[h, flip, 0].astype(f32)
                + near_ir[h, flip, 1].astype(f32)
            )

        fars1 = far(1)
        nears1 = near(1)
        yield
        fars0 = far(0)
        relay(1, fars1, nears1)
        nears0 = near(0)
        yield
        for copy in nears1:
            copy.wait_recv()
        y_is[h] = line_sum(1).astype(bf16)
        last = send(y_is.at[h], y_ir.at[h], y_next)
        relay(0, fars0, nears0)
        yield
        for copy in nears0 + [last]:
            copy.wait_recv()
        gout[:, mine] = line_sum(0) + y_ir[h].astype(f32)
        stores.append(fetch(gout.at[:, mine], grad_in.at[:, mine]))

    def once(stage, *args):
        stage(*args)
        yield

    first_a, first_b = first_norm(0), first_norm(1)
    feat_a, feat_b = gather_feat(0), gather_feat(1)
    norm_a, norm_b = second_norm(0), second_norm(1)
    dp_a, dp_b = gather_dp(0), gather_dp(1)
    gram_a, gram_b = sum_gram(0), sum_gram(1)
    back_a, back_b = output_back(0), output_back(1)
    act_a0, act_a1, act_b0, act_b1 = (active_back(v, h) for v in range(2) for h in range(2))
    pre_0, pre_1 = first_back(0), first_back(1)
    last_0, last_1 = last_layer(0), last_layer(1)
    loss, row = once(losses), once(row_losses)
    turn = once(transpose_emb)
    order = (
        first_a, first_a, feat_a, first_b, turn, feat_a, feat_a, feat_a, feat_b,
        feat_a, feat_a, norm_a, feat_b, norm_a, dp_a, feat_b, dp_a, feat_b, dp_a, feat_b, feat_b,
        norm_b, dp_a, norm_b, dp_a, dp_b, dp_a, gram_a, dp_b, gram_a, dp_b, gram_a, dp_b,
        gram_a, gram_a, dp_b, gram_a, gram_a, dp_b, loss,
        gram_b, back_b, gram_b, back_b, act_b0, gram_b, gram_b, gram_b, act_b0, gram_b, gram_b,
        back_a, act_b0, act_b1, back_a, act_b0, act_a0, act_b1, act_b0, act_b1, pre_0, act_a0,
        act_b1, act_a0, act_a1, act_b1, act_a0, act_a1, act_a0, pre_0, pre_1, act_a1, pre_0,
        last_0, act_a1, last_0, row, act_a1, pre_1, last_0, last_0, pre_1, last_1, last_0,
        last_1, last_1, last_1, last_1,
    )
    first_layer()
    for stage in order:
        next(stage, None)
    for stage in order:
        for _ in stage:
            raise ValueError()
    for copy in stores:
        copy.wait()
    for sender in senders:
        sender.finish()


def copies(*refs):
    for i in range(5):
        refs[5 + i][...] = refs[i][...]


def scratch():
    v = pltpu.VMEM
    return [
        v((2 * ROWS, EMB), bf16), v((EMB, WIDE), bf16), v((FEAT * WIDE, WIDE), bf16),
        v((2, WIDE), f32), v((4, WIDE), f32), v((2, ROWS, WIDE), f32), v((2, FEAT, ROWS, WIDE), bf16),
        v((2, ROWS, WIDE), f32),
        v((DP, 4, WIDE), f32), v((2, DP, 2, WIDE), f32),
        v((2, DP, 2, WIDE), f32), v((2, DP, 4, PIECE), f32),
        v((2, DP, ROWS, WIDE), bf16), v((DP, WIDE), f32),
        v((2, ROWS, BATCH), bf16), v((2, 2, 32, BATCH // 2), bf16),
        v((2, 2, 32, BATCH), bf16), v((2, 2, 32, BATCH), bf16),
        v((2, 16, BATCH), bf16), v((2, 16, BATCH), bf16), v((2, ROWS, BATCH), bf16),
        v((2, ROWS, WIDE), bf16),
        v((2, 2, 2, ROWS, PIECE), bf16), v((2, 2, 2, 2, HALF, PIECE), bf16),
        v((2, 2, 2, 2, ROWS, PIECE), bf16), v((2, 2, 2, 2, ROWS, PIECE), bf16),
        v((2, 2, ROWS, PIECE), bf16), v((2, 2, ROWS, PIECE), bf16), v((2, ROWS, WIDE), f32),
        v((2 * ROWS, WIDE), bf16), v((EMB, 2 * ROWS), bf16),
        v((2, 8, OUT, PIECE), bf16),
        v((2, 2, OUT, PIECE), bf16), v((2, 2, 2, OUT // 2, PIECE), bf16),
        v((2, 2, 2, OUT, PIECE), bf16), v((2, 2, 2, OUT, PIECE), bf16),
        v((2, OUT, PIECE), bf16), v((2, OUT, PIECE), bf16), v((OUT, WIDE), f32),
        pltpu.SemaphoreType.DMA((20,)), pltpu.SemaphoreType.DMA((186,)),
        pltpu.SemaphoreType.DMA((8,)),
    ]


def shards(emb_a, emb_b, w_in, w_out, gain, shift):
    anywhere = pl.BlockSpec(memory_space=pl.ANY)
    near = pl.BlockSpec(memory_space=pltpu.VMEM)
    results = pl.pallas_call(
        kernel,
        out_shape=(
            jax.ShapeDtypeStruct((OUT, WIDE), f32),
            jax.ShapeDtypeStruct((1, WIDE), f32),
            jax.ShapeDtypeStruct((1, WIDE), f32),
            jax.ShapeDtypeStruct((1, WIDE), f32),
            jax.ShapeDtypeStruct((1, ROWS), f32),
        ),
        in_specs=[anywhere] * 6,
        out_specs=(anywhere, near, near, near, near),
        scratch_shapes=scratch(),
        compiler_params=pltpu.CompilerParams(
            collective_id=0, has_side_effects=True, vmem_limit_bytes=62 * 2**20
        ),
        cost_estimate=pl.CostEstimate(flops=14 * 10**9, bytes_accessed=24 * 2**20, transcendentals=0),
    )(emb_a, emb_b, w_in, w_out, gain.reshape(1, WIDE), shift.reshape(1, WIDE))
    results = pl.pallas_call(
        copies,
        out_shape=tuple(jax.ShapeDtypeStruct(r.shape, r.dtype) for r in results),
        in_specs=[near] * 5,
        out_specs=(near,) * 5,
    )(*results)
    return (results[0],) + tuple(r.reshape(-1) for r in results[1:])


def solution(mesh):
    return jax.shard_map(
        shards,
        mesh=mesh,
        in_specs=(
            P("dp", None), P("dp", None), P(None, "feat"), P(None, "feat"), P("feat"), P("feat"),
        ),
        out_specs=(P("dp", "feat"), P("feat"), P("feat"), P("feat"), P("dp")),
        check_vma=False,
    )
```

```python
import functools
import math

import jax
import jax.numpy as jnp
from jax import lax
from jax.experimental import pallas as pl
from jax.experimental.pallas import tpu as pltpu
from jax.sharding import PartitionSpec as P

MESH = pl.DeviceIdType.MESH
epsilon = 1e-05
off_weight = 0.0051
BATCH = 2048
ROWS = 128
WIDE = 1024
EMB = 1536
DP = 16
FEAT = 8
OUT = EMB // DP
TILE = 256
PIECE = WIDE // 2
HALF = ROWS // 2
FEAT_EDGE = (HALF, HALF)
DP_EDGE = (HALF, HALF)
BACK_EDGE = ((48, 48), (48, 48))
f32 = jnp.float32
bf16 = jnp.bfloat16
NT = (((1,), (1,)), ((), ()))


def column_tiles(body, width=WIDE, tile=TILE):
    @pl.loop(0, width // tile)
    def _(i):
        body(pl.ds(pl.multiple_of(i * tile, tile), tile))


def kernel(
    emb_a, emb_b, w_in, w_out, gain, shift,
    grad_in, grad_gain, grad_shift, diag_loss, row_loss,
    emb, win, wout, gn_sh, inv, hid, act, out, st1, st2, st3, st4, nrm, corr,
    part, far_g, near_gs, near_gr, y_gs, y_gr, gram, go,
    far_s, far_r, near_s, near_r, ys, yr, cross_s, cross_r, gact, gh, emb_t,
    core_r, far_is, far_ir, near_is, near_ir, y_is, y_ir, gout,
    send_sem, recv_sem, local_sem,
):
    dp, ft = lax.axis_index("dp"), lax.axis_index("feat")
    core, z = lax.rem(dp, 2), lax.rem(dp // 2, 4)
    y_lo, x, y_hi = dp // 8, ft // 2, lax.rem(ft, 2)

    def at_x(step):
        return lax.rem(x + step + 4, 4)

    def at_z(step):
        return lax.rem(z + step + 4, 4)

    def feat_of(step, flip=0):
        return at_x(step) * 2 + (y_hi + flip * (1 - 2 * y_hi))

    def dp_of(step, flip_y=0, flip_core=0):
        yy = y_lo + flip_y * (1 - 2 * y_lo)
        return (yy * 4 + at_z(step)) * 2 + (core + flip_core * (1 - 2 * core))

    x_right, x_left, y_pair = (dp, feat_of(1)), (dp, feat_of(-1)), (dp, feat_of(0, 1))
    z_right, z_left = (dp_of(1), ft), (dp_of(-1), ft)
    y_next, other = (dp_of(0, 1), ft), (dp_of(0, 0, 1), ft)
    peers = [(lax.rem(dp + k, DP), ft) for k in range(1, DP)]

    waiting = []
    counts = [0, 0, 0]

    def size(ref):
        return math.prod(ref.shape) * jnp.dtype(ref.dtype).itemsize

    def all_of(sem, total):
        count = total // (16 * 2 * WIDE)
        ref = wout.at[pl.ds(0, 16 * count)]
        return pltpu.make_async_copy(ref, ref, sem)

    class Sender:
        def __init__(self):
            self.sem = send_sem.at[counts[2]]
            counts[2] += 1
            self.total = 0
            senders.append(self)

        def __call__(self, src, dst, device):
            i = counts[0]
            counts[0] += 1
            copy = pltpu.make_async_remote_copy(
                src_ref=src, dst_ref=dst, send_sem=self.sem, recv_sem=recv_sem.at[i],
                device_id=device, device_id_type=MESH,
            )
            copy.start()
            self.total += size(src)
            return copy

        def finish(self):
            all_of(self.sem, self.total).wait()

    senders = []

    class Share:
        def __init__(self, table):
            self.leave, self.land = send_sem.at[counts[2]], recv_sem.at[counts[0]]
            counts[2] += 1
            counts[0] += 1
            for device in peers:
                pltpu.make_async_remote_copy(
                    src_ref=table.at[dp], dst_ref=table.at[dp], send_sem=self.leave,
                    recv_sem=self.land, device_id=device, device_id_type=MESH,
                ).start()
            self.others = table.at[pl.ds(0, DP - 1)]
            senders.append(self)

        def wait_recv(self):
            pltpu.make_async_copy(self.others, self.others, self.land).wait()

        def finish(self):
            pltpu.make_async_copy(self.others, self.others, self.leave).wait()

    def fetch(src, dst):
        i = counts[1]
        counts[1] += 1
        copy = pltpu.make_async_copy(src, dst, local_sem.at[i])
        copy.start()
        return copy

    in_emb = [fetch(emb_a, emb.at[pl.ds(0, ROWS)]), fetch(emb_b, emb.at[pl.ds(ROWS, ROWS)])]
    in_win = fetch(w_in, win)
    in_gs = [fetch(gain, gn_sh.at[pl.ds(0, 1)]), fetch(shift, gn_sh.at[pl.ds(1, 1)])]

    barrier = pltpu.get_barrier_semaphore()
    greeted = peers + [x_right, x_left, y_pair]
    for device in greeted:
        pl.semaphore_signal(barrier, inc=1, device_id=device, device_id_type=MESH)

    def rows(v):
        return pl.ds(v * ROWS, ROWS)

    def local_moments(values, table, row, cols):
        center = jnp.sum(values, axis=0, keepdims=True) / ROWS
        spread = jnp.sum((values - center) ** 2, axis=0, keepdims=True)
        table[dp, row : row + 1, cols] = center
        table[dp, row + 1 : row + 2, cols] = spread

    def global_moments(table, row, cols):
        centers = table[:, row, cols]
        center = jnp.sum(centers, axis=0, keepdims=True) / DP
        spread = jnp.sum(table[:, row + 1, cols], axis=0, keepdims=True) + ROWS * jnp.sum(
            (centers - center) ** 2, axis=0, keepdims=True
        )
        return center, lax.rsqrt(spread / BATCH + epsilon)

    def first_layer():
        for copy in in_emb:
            copy.wait()
        in_win.wait()
        waiting.append(fetch(w_out, wout))

        def tile(cols):
            product = jnp.dot(emb[...], win[:, cols], preferred_element_type=f32)
            for v in range(2):
                piece = product[v * ROWS : (v + 1) * ROWS]
                hid[v, :, cols] = piece
                local_moments(piece, st1, 2 * v, cols)

        column_tiles(tile)
        pl.semaphore_wait(barrier, len(greeted))

    def first_norm(v):
        if v == 0:
            exchange = Share(st1)
            yield
            exchange.wait_recv()
            for copy in in_gs:
                copy.wait()

        def tile(cols):
            center, inverse = global_moments(st1, 2 * v, cols)
            hat = (hid[v, :, cols] - center) * inverse
            hid[v, :, cols] = hat
            inv[v : v + 1, cols] = inverse
            before = gn_sh[0:1, cols] * hat + gn_sh[1:2, cols]
            act[v, ft, :, cols] = jnp.maximum(before, 0.0).astype(bf16)

        column_tiles(tile)
        yield

    def project(v, slot, first=False):
        def tile(cols):
            product = jnp.dot(
                act[v, slot], wout[pl.ds(pl.multiple_of(slot * WIDE, WIDE), WIDE), cols],
                preferred_element_type=f32,
            )
            if first:
                out[v, :, cols] = product
            else:
                out[v, :, cols] += product

        column_tiles(tile)

    def gather(buffer, slot, right, left, pair, edge, have):
        send = Sender()
        low, high = pl.ds(0, HALF), pl.ds(HALF, HALF)
        top, bottom = pl.ds(0, edge), pl.ds(ROWS - edge, edge)
        middle = pl.ds(edge, ROWS - 2 * edge)
        split = edge < HALF

        def go_(block, device, part_rows=None):
            ref = buffer.at[block] if part_rows is None else buffer.at[block, part_rows]
            return send(ref, ref, device)

        def arrive(*copies):
            for copy in copies:
                copy.wait_recv()

        a = go_(slot(0, 0), pair)
        b = go_(slot(0, 0), right)
        c = go_(slot(0, 0), left)
        have(0, 0)
        yield
        arrive(a)
        parts = (top, bottom) if split else (None,)
        d = [go_(slot(0, 1), right, part_rows) for part_rows in parts]
        e = [go_(slot(0, 1), left, part_rows) for part_rows in parts[::-1]]
        have(0, 1)
        yield
        late = []
        arrive(b)
        f = go_(slot(-1, 0), right, low)
        if split:
            late.append(go_(slot(-1, 0), pair, middle))
        arrive(c)
        g = go_(slot(1, 0), left, high)
        if split:
            late.append(go_(slot(1, 0), pair, middle))
        have(-1, 0)
        have(1, 0)
        yield
        arrive(d[0])
        h = go_(slot(-1, 1), right, top)
        arrive(e[0])
        i = go_(slot(1, 1), left, bottom)
        arrive(*d[1:], *e[1:], *late)
        have(-1, 1)
        have(1, 1)
        yield
        arrive(f, g)
        late = [go_(slot(2, 0), pair, middle)] if split else []
        have(2, 0)
        yield
        arrive(h, i, *late)
        have(2, 1)

    def gather_feat(v):
        def have(step, flip):
            if v == 0 and waiting:
                waiting.pop().wait()
            project(v, feat_of(step, flip), first=step == 0 and flip == 0)

        return gather(act.at[v], feat_of, x_right, x_left, y_pair, FEAT_EDGE[v], have)

    def second_norm(v):
        column_tiles(lambda cols: local_moments(out[v, :, cols], st2.at[v], 0, cols))
        exchange = Share(st2.at[v])
        yield
        exchange.wait_recv()

        def tile(cols):
            center, inverse = global_moments(st2.at[v], 0, cols)
            hat = (out[v, :, cols] - center) * inverse
            out[v, :, cols] = hat
            inv[2 + v : 3 + v, cols] = inverse
            nrm[v, dp, :, cols] = hat.astype(bf16)

        column_tiles(tile)

    def inner(v, slot):
        cols = pl.ds(pl.multiple_of(slot * ROWS, ROWS), ROWS)
        part[v, :, cols] = lax.dot_general(
            nrm[v, dp], nrm[v, slot], NT, preferred_element_type=f32
        ).astype(bf16)
        if v == 1:
            corr[pl.ds(slot, 1), :] = jnp.sum(
                nrm[0, slot].astype(f32) * nrm[1, slot].astype(f32), axis=0, keepdims=True
            )

    def gather_dp(v):
        send = Sender()
        cores = []

        def from_core(count):
            for _ in range(count):
                copy, step, flip = cores.pop(0)
                copy.wait_recv()
                inner(v, dp_of(step, flip, 1))

        def have(step, flip):
            slot = dp_of(step, flip)
            cores.append((send(nrm.at[v, slot], nrm.at[v, slot], other), step, flip))
            inner(v, slot)
            if (step, flip) not in ((0, 0), (-1, 0), (-1, 1)):
                from_core(len(cores) if (step, flip) == (2, 1) else len(cores) - 1)

        return gather(nrm.at[v], dp_of, z_right, z_left, y_next, DP_EDGE[v], have)

    def sum_gram(v):
        send = Sender()
        low, high = pl.ds(0, BATCH // 2), pl.ds(BATCH // 2, BATCH // 2)

        def pair_rows(step):
            return pl.ds(pl.multiple_of(at_x(step) * 32, 32), 32)

        far_right = send(part.at[v, pair_rows(2), low], far_g.at[v, 0], x_right)
        far_left = send(part.at[v, pair_rows(2), high], far_g.at[v, 1], x_left)
        near_gs[v, 0] = part[v, pair_rows(1), :]
        near_gs[v, 1] = part[v, pair_rows(-1), :]
        near = [
            send(near_gs.at[v, 0, :, high], near_gr.at[v, 0, :, high], x_right),
            send(near_gs.at[v, 1, :, low], near_gr.at[v, 1, :, low], x_left),
        ]
        yield
        far_right.wait_recv()
        near_gs[v, 0, :, low] = (
            near_gs[v, 0, :, low].astype(f32) + far_g[v, 0].astype(f32)
        ).astype(bf16)
        near.append(send(near_gs.at[v, 0, :, low], near_gr.at[v, 0, :, low], x_right))
        far_left.wait_recv()
        near_gs[v, 1, :, high] = (
            near_gs[v, 1, :, high].astype(f32) + far_g[v, 1].astype(f32)
        ).astype(bf16)
        near.append(send(near_gs.at[v, 1, :, high], near_gr.at[v, 1, :, high], x_left))
        yield
        for copy in near:
            copy.wait_recv()

        def line_sum(flip):
            h = y_hi + flip * (1 - 2 * y_hi)
            block = pl.ds(pl.multiple_of(h * 16, 16), 16)
            return (
                part[v, pl.ds(pl.multiple_of(feat_of(0, flip) * 16, 16), 16), :].astype(f32)
                + near_gr[v, 0, block, :].astype(f32)
                + near_gr[v, 1, block, :].astype(f32)
            )

        y_gs[v] = line_sum(1).astype(bf16)
        a = send(y_gs.at[v], y_gr.at[v], y_pair)
        yield
        a.wait_recv()

        def slot(step, flip=0):
            return pl.ds(pl.multiple_of(feat_of(step, flip) * 16, 16), 16)

        gram[v, slot(0), :] = (line_sum(0) + y_gr[v].astype(f32)).astype(bf16)

        def go_(block, device, cols=None):
            ref = gram.at[v, block] if cols is None else gram.at[v, block, cols]
            return send(ref, ref, device)

        a = go_(slot(0), y_pair)
        b = go_(slot(0), x_right)
        c = go_(slot(0), x_left)
        yield
        a.wait_recv()
        d = go_(slot(0, 1), x_right)
        e = go_(slot(0, 1), x_left)
        yield
        b.wait_recv()
        f = go_(slot(-1), x_right, low)
        c.wait_recv()
        g = go_(slot(1), x_left, high)
        yield
        d.wait_recv()
        h = go_(slot(-1, 1), x_right, low)
        e.wait_recv()
        i = go_(slot(1, 1), x_left, high)
        yield
        for copy in (f, g, h, i):
            copy.wait_recv()

    factor = BATCH / 64.0
    coeff = 2.0 * off_weight / (BATCH * BATCH)

    def losses():
        diag = jnp.sum(corr[...], axis=0, keepdims=True) / BATCH
        diag_loss[...] = (1.0 - diag) ** 2 - off_weight * diag**2
        corr[0:1, :] = -2.0 * (1.0 - diag) - 2.0 * off_weight * diag

    def row_losses():
        total = jnp.zeros((ROWS, ROWS), f32)
        for k in range(BATCH // ROWS):
            cols = slice(k * ROWS, (k + 1) * ROWS)
            total += gram[0, :, cols].astype(f32) * gram[1, :, cols].astype(f32)
        total = jnp.sum(total.T, axis=0, keepdims=True)
        row_loss[...] = total / (BATCH * WIDE * FEAT)

    def output_back(v):
        def tile(cols):
            product = jnp.dot(
                gram[1 - v], nrm[v, :, :, cols].reshape(BATCH, TILE), preferred_element_type=f32
            )
            upstream = factor * (
                coeff * product + nrm[1 - v, dp, :, cols].astype(f32) * corr[0:1, cols] / BATCH
            )
            gact[v, :, cols] = upstream
            st3[v, dp, 0:1, cols] = jnp.sum(upstream, axis=0, keepdims=True)
            st3[v, dp, 1:2, cols] = jnp.sum(upstream * out[v, :, cols], axis=0, keepdims=True)

        column_tiles(tile)
        exchange = Share(st3.at[v])
        yield
        exchange.wait_recv()

        def finish(cols):
            up = jnp.sum(st3[v, :, 0, cols], axis=0, keepdims=True) / BATCH
            dot = jnp.sum(st3[v, :, 1, cols], axis=0, keepdims=True) / BATCH
            go[v, :, cols] = (
                inv[2 + v : 3 + v, cols] * (gact[v, :, cols] - up - out[v, :, cols] * dot)
            ).astype(bf16)

        column_tiles(finish)

    def keep(ref):
        def store(cols, value):
            ref[:, cols] = value.astype(bf16)

        return store

    stores = []

    def active_back(v, h):
        send = Sender()
        def block(step, flip, store):
            first = feat_of(step, flip) * WIDE + h * PIECE

            def tile(cols):
                store(
                    cols,
                    lax.dot_general(
                        go[v], wout[pl.ds(pl.multiple_of(first + cols.start, TILE), TILE), :], NT,
                        preferred_element_type=f32,
                    ),
                )

            column_tiles(tile, PIECE)

        edge = BACK_EDGE[v][h]
        top, bottom = pl.ds(0, edge), pl.ds(ROWS - edge, edge)
        middle, between = pl.ds(edge, ROWS - 2 * edge), pl.ds(0, ROWS - 2 * edge)
        mine = pl.ds(h * PIECE, PIECE)
        crossed = {}

        def cross(step, ref):
            slot = (2, 1, -1, 0).index(step)
            crossed[step] = send(ref, cross_r.at[v, h, slot, between], y_pair)

        def added(step, ref):
            slot = (2, 1, -1, 0).index(step)
            crossed[step].wait_recv()

            def store(cols, value):
                ref[:, cols] = value.astype(bf16)
                ref[middle, cols] = (
                    value[edge : ROWS - edge] + cross_r[v, h, slot, between, cols].astype(f32)
                ).astype(bf16)

            return store

        def far(flip):
            ref = far_s.at[v, h, flip]
            block(2, flip, keep(ref) if flip else added(2, ref))
            if flip:
                cross(2, ref.at[middle])
            first, second = (top, bottom) if flip else (low, high)
            into = between_half if not flip else pl.ds(0, edge)
            return [
                send(ref.at[first], far_r.at[v, h, flip, 0, into], x_right),
                send(ref.at[second], far_r.at[v, h, flip, 1, into], x_left),
            ]

        low, high = pl.ds(0, HALF), pl.ds(HALF, HALF)
        between_half = pl.ds(0, HALF)

        def near(flip):
            first, second = (top, bottom) if flip else (low, high)
            copies = []
            for side, step, part_rows, device in ((0, 1, second, x_right), (1, -1, first, x_left)):
                ref = near_s.at[v, h, flip, side]
                block(step, flip, keep(ref) if flip else added(step, ref))
                copies.append(
                    send(ref.at[part_rows], near_r.at[v, h, flip, side, part_rows], device)
                )
                if flip:
                    cross(step, ref.at[middle])
            return copies

        def relay(flip, fars, nears):
            first, second = (top, bottom) if flip else (low, high)
            into = between_half if not flip else pl.ds(0, edge)
            for side, part_rows, device in ((0, first, x_right), (1, second, x_left)):
                fars[side].wait_recv()
                near_s[v, h, flip, side, part_rows] = (
                    near_s[v, h, flip, side, part_rows].astype(f32)
                    + far_r[v, h, flip, side, into].astype(f32)
                ).astype(bf16)
                nears.append(
                    send(
                        near_s.at[v, h, flip, side, part_rows],
                        near_r.at[v, h, flip, side, part_rows], device,
                    )
                )

        def store_own(cols, value):
            gact[v, :, pl.ds(pl.multiple_of(h * PIECE + cols.start, TILE), TILE)] = value

        def store_pair(cols, value):
            store_own(cols, value)
            cross_s[v, h, between, cols] = value[edge : ROWS - edge].astype(bf16)

        fars1 = far(1)
        yield
        nears1 = near(1)
        yield
        block(0, 1, store_pair)
        cross(0, cross_s.at[v, h, between])
        yield
        fars0 = far(0)
        yield
        relay(1, fars1, nears1)
        yield
        nears0 = near(0)
        yield
        for copy in nears1:
            copy.wait_recv()
        for place, part_rows in ((pl.ds(0, edge), top), (pl.ds(edge, edge), bottom)):
            ys[v, h, place] = (
                gact[v, part_rows, mine]
                + near_r[v, h, 1, 0, part_rows].astype(f32)
                + near_r[v, h, 1, 1, part_rows].astype(f32)
            ).astype(bf16)
        edges = pl.ds(0, 2 * edge)
        last = send(ys.at[v, h, edges], yr.at[v, h, edges], y_pair)
        yield
        block(0, 0, store_own)
        yield
        relay(0, fars0, nears0)
        yield
        for copy in nears0 + [last, crossed[0]]:
            copy.wait_recv()

    def first_back(h):
        def tile(v, cols):
            edge = BACK_EDGE[v][h]
            full = pl.ds(pl.multiple_of(h * PIECE + cols.start, TILE), TILE)
            hat = hid[v, :, full]
            grad = (
                gact[v, :, full]
                + near_r[v, h, 0, 0, :, cols].astype(f32)
                + near_r[v, h, 0, 1, :, cols].astype(f32)
                + jnp.concatenate(
                    [
                        yr[v, h, 0:edge, cols],
                        cross_r[v, h, 3, 0 : ROWS - 2 * edge, cols],
                        yr[v, h, edge : 2 * edge, cols],
                    ]
                ).astype(f32)
            )
            before = gn_sh[0:1, full] * hat + gn_sh[1:2, full]
            grad = jnp.where(before > 0, grad, 0.0)
            gact[v, :, full] = grad
            st4[h, dp, 2 * v : 2 * v + 1, cols] = jnp.sum(grad, axis=0, keepdims=True)
            st4[h, dp, 2 * v + 1 : 2 * v + 2, cols] = jnp.sum(grad * hat, axis=0, keepdims=True)

        column_tiles(functools.partial(tile, 1), PIECE)
        yield
        column_tiles(functools.partial(tile, 0), PIECE)
        exchange = Share(st4.at[h])
        yield
        exchange.wait_recv()

        def finish(cols):
            full = pl.ds(pl.multiple_of(h * PIECE + cols.start, TILE), TILE)
            sums = [jnp.sum(st4[h, :, k, cols], axis=0, keepdims=True) for k in range(4)]
            for v in range(2):
                up, dot = sums[2 * v], sums[2 * v + 1]
                gh[rows(v), full] = (
                    gn_sh[0:1, full] * inv[v : v + 1, full]
                    * (gact[v, :, full] - up / BATCH - hid[v, :, full] * (dot / BATCH))
                ).astype(bf16)
            grad_shift[:, full] = sums[0] + sums[2]
            grad_gain[:, full] = sums[1] + sums[3]

        column_tiles(finish, PIECE)

    def transpose_emb():
        for k in range(EMB // ROWS):
            cols = slice(k * ROWS, (k + 1) * ROWS)
            emb_t[cols, :] = emb[:, cols].T

    def last_layer(h):
        send = Sender()
        low, high = pl.ds(0, OUT // 2), pl.ds(OUT // 2, OUT // 2)
        mine = pl.ds(h * PIECE, PIECE)

        def product(cols):
            full = pl.ds(pl.multiple_of(h * PIECE + cols.start, TILE), TILE)
            win[:, full] = jnp.dot(
                emb_t[...], gh[:, full], preferred_element_type=f32
            ).astype(bf16)

        def block(step, flip_y, flip_core):
            target = dp_of(step, flip_y, flip_core)
            return win.at[pl.ds(pl.multiple_of(target * OUT, OUT), OUT), mine]

        column_tiles(product, PIECE)
        order = [(2, 1), (1, 1), (-1, 1), (2, 0), (1, 0), (-1, 0), (0, 1), (0, 0)]
        crossing = {}
        for n, (step, flip) in enumerate(order):
            crossing[step, flip] = send(block(step, flip, 1), core_r.at[h, n], other)
        yield

        def chip_sum(step, flip):
            n = order.index((step, flip))
            crossing[step, flip].wait_recv()
            return block(step, flip, 0)[...].astype(f32) + core_r[h, n].astype(f32)

        def far(flip):
            far_is[h, flip] = chip_sum(2, flip).astype(bf16)
            return [
                send(far_is.at[h, flip, low], far_ir.at[h, flip, 0], z_right),
                send(far_is.at[h, flip, high], far_ir.at[h, flip, 1], z_left),
            ]

        def near(flip):
            near_is[h, flip, 0] = chip_sum(1, flip).astype(bf16)
            a = send(near_is.at[h, flip, 0, high], near_ir.at[h, flip, 0, high], z_right)
            near_is[h, flip, 1] = chip_sum(-1, flip).astype(bf16)
            b = send(near_is.at[h, flip, 1, low], near_ir.at[h, flip, 1, low], z_left)
            return [a, b]

        def relay(flip, fars, nears):
            for side, half, device in ((0, low, z_right), (1, high, z_left)):
                fars[side].wait_recv()
                near_is[h, flip, side, half] = (
                    near_is[h, flip, side, half].astype(f32) + far_ir[h, flip, side].astype(f32)
                ).astype(bf16)
                nears.append(
                    send(near_is.at[h, flip, side, half], near_ir.at[h, flip, side, half], device)
                )

        def line_sum(flip):
            return (
                chip_sum(0, flip)
                + near_ir[h, flip, 0].astype(f32)
                + near_ir[h, flip, 1].astype(f32)
            )

        fars1 = far(1)
        nears1 = near(1)
        yield
        fars0 = far(0)
        yield
        relay(1, fars1, nears1)
        yield
        nears0 = near(0)
        yield
        for copy in nears1:
            copy.wait_recv()
        y_is[h] = line_sum(1).astype(bf16)
        last = send(y_is.at[h], y_ir.at[h], y_next)
        yield
        relay(0, fars0, nears0)
        yield
        for copy in nears0 + [last]:
            copy.wait_recv()
        gout[:, mine] = line_sum(0) + y_ir[h].astype(f32)
        stores.append(fetch(gout.at[:, mine], grad_in.at[:, mine]))

    def once(stage, *args):
        stage(*args)
        yield

    first_a, first_b = first_norm(0), first_norm(1)
    feat_a, feat_b = gather_feat(0), gather_feat(1)
    norm_a, norm_b = second_norm(0), second_norm(1)
    dp_a, dp_b = gather_dp(0), gather_dp(1)
    gram_a, gram_b = sum_gram(0), sum_gram(1)
    back_a, back_b = output_back(0), output_back(1)
    act_a0, act_a1, act_b0, act_b1 = (active_back(v, h) for v in range(2) for h in range(2))
    pre_0, pre_1 = first_back(0), first_back(1)
    last_0, last_1 = last_layer(0), last_layer(1)
    loss, row = once(losses), once(row_losses)
    turn = once(transpose_emb)
    order = (
        first_a, first_a, feat_a, feat_a, first_b, feat_a, feat_a, feat_b, feat_a, turn, feat_a,
        norm_a, feat_b, norm_a, dp_a, feat_b, feat_b, dp_a, dp_a, feat_b, feat_b, norm_b, dp_a,
        dp_a, norm_b, dp_b, dp_a, gram_a, gram_a, dp_b, gram_a, dp_b, gram_a, dp_b, gram_a, dp_b,
        dp_b, gram_b, gram_a, gram_b, loss, gram_a, gram_b, gram_a, back_b, gram_b, back_b, act_b1,
        gram_b, act_b0, act_b0, act_b1, gram_b, act_b0, act_b1, gram_b, act_b1, act_b1, act_b0,
        act_b0, act_b0, act_b1, gram_b, back_a, act_b1, act_b1, act_b1, act_b0, act_b0, act_b0,
        back_a, act_a1, act_a0, act_a1, act_a0, act_b1, act_a0, act_a1, act_a1, act_a1, act_a0,
        act_a0, act_b0, row, act_a1, pre_1, act_a1, act_a1, act_a1, act_a0, act_a0, act_a0, act_a0,
        act_a1, pre_1, pre_0, act_a0, pre_0, pre_1, last_1, pre_0, last_1, last_0, last_1, last_0,
        last_1, last_0, last_0, last_1, last_0, last_1, last_1, last_0, last_0, last_1, last_0,
    )
    first_layer()
    for stage in order:
        next(stage, None)
    for stage in order:
        for _ in stage:
            raise ValueError()
    for copy in stores:
        copy.wait()
    for sender in senders:
        sender.finish()


def copies(*refs):
    for i in range(5):
        refs[5 + i][...] = refs[i][...]


def scratch():
    v = pltpu.VMEM
    return [
        v((2 * ROWS, EMB), bf16), v((EMB, WIDE), bf16), v((FEAT * WIDE, WIDE), bf16),
        v((2, WIDE), f32), v((4, WIDE), f32), v((2, ROWS, WIDE), f32), v((2, FEAT, ROWS, WIDE), bf16),
        v((2, ROWS, WIDE), f32),
        v((DP, 4, WIDE), f32), v((2, DP, 2, WIDE), f32),
        v((2, DP, 2, WIDE), f32), v((2, DP, 4, PIECE), f32),
        v((2, DP, ROWS, WIDE), bf16), v((DP, WIDE), f32),
        v((2, ROWS, BATCH), bf16), v((2, 2, 32, BATCH // 2), bf16),
        v((2, 2, 32, BATCH), bf16), v((2, 2, 32, BATCH), bf16),
        v((2, 16, BATCH), bf16), v((2, 16, BATCH), bf16), v((2, ROWS, BATCH), bf16),
        v((2, ROWS, WIDE), bf16),
        v((2, 2, 2, ROWS, PIECE), bf16), v((2, 2, 2, 2, HALF, PIECE), bf16),
        v((2, 2, 2, 2, ROWS, PIECE), bf16), v((2, 2, 2, 2, ROWS, PIECE), bf16),
        v((2, 2, ROWS, PIECE), bf16), v((2, 2, ROWS, PIECE), bf16),
        v((2, 2, HALF, PIECE), bf16), v((2, 2, 4, HALF, PIECE), bf16), v((2, ROWS, WIDE), f32),
        v((2 * ROWS, WIDE), bf16), v((EMB, 2 * ROWS), bf16),
        v((2, 8, OUT, PIECE), bf16),
        v((2, 2, OUT, PIECE), bf16), v((2, 2, 2, OUT // 2, PIECE), bf16),
        v((2, 2, 2, OUT, PIECE), bf16), v((2, 2, 2, OUT, PIECE), bf16),
        v((2, OUT, PIECE), bf16), v((2, OUT, PIECE), bf16), v((OUT, WIDE), f32),
        pltpu.SemaphoreType.DMA((21,)), pltpu.SemaphoreType.DMA((216,)),
        pltpu.SemaphoreType.DMA((8,)),
    ]


def shards(emb_a, emb_b, w_in, w_out, gain, shift):
    anywhere = pl.BlockSpec(memory_space=pl.ANY)
    near = pl.BlockSpec(memory_space=pltpu.VMEM)
    results = pl.pallas_call(
        kernel,
        out_shape=(
            jax.ShapeDtypeStruct((OUT, WIDE), f32),
            jax.ShapeDtypeStruct((1, WIDE), f32),
            jax.ShapeDtypeStruct((1, WIDE), f32),
            jax.ShapeDtypeStruct((1, WIDE), f32),
            jax.ShapeDtypeStruct((1, ROWS), f32),
        ),
        in_specs=[anywhere] * 6,
        out_specs=(anywhere, near, near, near, near),
        scratch_shapes=scratch(),
        compiler_params=pltpu.CompilerParams(
            collective_id=0, has_side_effects=True, vmem_limit_bytes=62 * 2**20
        ),
        cost_estimate=pl.CostEstimate(flops=14 * 10**9, bytes_accessed=24 * 2**20, transcendentals=0),
    )(emb_a, emb_b, w_in, w_out, gain.reshape(1, WIDE), shift.reshape(1, WIDE))
    results = pl.pallas_call(
        copies,
        out_shape=tuple(jax.ShapeDtypeStruct(r.shape, r.dtype) for r in results),
        in_specs=[near] * 5,
        out_specs=(near,) * 5,
    )(*results)
    return (results[0],) + tuple(r.reshape(-1) for r in results[1:])


def solution(mesh):
    return jax.shard_map(
        shards,
        mesh=mesh,
        in_specs=(
            P("dp", None), P("dp", None), P(None, "feat"), P(None, "feat"), P("feat"), P("feat"),
        ),
        out_specs=(P("dp", "feat"), P("feat"), P("feat"), P("feat"), P("dp")),
        check_vma=False,
    )
```

```python
import functools
import math

import jax
import jax.numpy as jnp
from jax import lax
from jax.experimental import pallas as pl
from jax.experimental.pallas import tpu as pltpu
from jax.sharding import PartitionSpec as P

MESH = pl.DeviceIdType.MESH
epsilon = 1e-05
off_weight = 0.0051
BATCH = 2048
ROWS = 128
WIDE = 1024
EMB = 1536
DP = 16
FEAT = 8
OUT = EMB // DP
TILE = 256
PIECES = (512, 512)
STARTS = (0, 512)
PIECE = max(PIECES)
HALF = ROWS // 2
FEAT_EDGE = (HALF, HALF)
DP_EDGE = (HALF, HALF)
BACK_EDGE = ((48, 48), (48, 48))
f32 = jnp.float32
bf16 = jnp.bfloat16
NT = (((1,), (1,)), ((), ()))


def column_tiles(body, width=WIDE, tile=TILE):
    @pl.loop(0, width // tile)
    def _(i):
        body(pl.ds(pl.multiple_of(i * tile, tile), tile))


def kernel(
    emb_a, emb_b, w_in, w_out, gain, shift,
    grad_in, grad_gain, grad_shift, diag_loss, row_loss,
    emb, win, wout, gn_sh, inv, hid, act, out, st1, st2, st3, st4, nrm, corr,
    part, sum_r, gram, go,
    far_s, far_r, near_s, near_r, ys, yr, cross_s, cross_r, gact, gh, emb_t,
    core_r, far_is, far_ir, near_is, near_ir, y_is, y_ir, gout,
    send_sem, recv_sem, local_sem,
):
    dp, ft = lax.axis_index("dp"), lax.axis_index("feat")
    core, z = lax.rem(dp, 2), lax.rem(dp // 2, 4)
    y_lo, x, y_hi = dp // 8, ft // 2, lax.rem(ft, 2)

    def at_x(step):
        return lax.rem(x + step + 4, 4)

    def at_z(step):
        return lax.rem(z + step + 4, 4)

    def feat_of(step, flip=0):
        return at_x(step) * 2 + (y_hi + flip * (1 - 2 * y_hi))

    def dp_of(step, flip_y=0, flip_core=0):
        yy = y_lo + flip_y * (1 - 2 * y_lo)
        return (yy * 4 + at_z(step)) * 2 + (core + flip_core * (1 - 2 * core))

    x_right, x_left, y_pair = (dp, feat_of(1)), (dp, feat_of(-1)), (dp, feat_of(0, 1))
    z_right, z_left = (dp_of(1), ft), (dp_of(-1), ft)
    y_next, other = (dp_of(0, 1), ft), (dp_of(0, 0, 1), ft)
    peers = [(lax.rem(dp + k, DP), ft) for k in range(1, DP)]
    places = [(2, 1), (1, 1), (-1, 1), (2, 0), (0, 1), (1, 0), (-1, 0)]
    members = [(place, (dp, feat_of(*place))) for place in places]

    waiting = []
    counts = [0, 0, 0]

    def size(ref):
        return math.prod(ref.shape) * jnp.dtype(ref.dtype).itemsize

    def all_of(sem, total):
        assert total % (16 * WIDE) == 0
        ref = wout.at[pl.ds(0, total // WIDE), pl.ds(0, WIDE // 2)]
        return pltpu.make_async_copy(ref, ref, sem)

    class Sender:
        def __init__(self):
            self.sem = send_sem.at[counts[2]]
            counts[2] += 1
            self.total = 0
            senders.append(self)

        def __call__(self, src, dst, device):
            i = counts[0]
            counts[0] += 1
            copy = pltpu.make_async_remote_copy(
                src_ref=src, dst_ref=dst, send_sem=self.sem, recv_sem=recv_sem.at[i],
                device_id=device, device_id_type=MESH,
            )
            copy.start()
            self.total += size(src)
            return copy

        def finish(self):
            all_of(self.sem, self.total).wait()

    senders = []

    class Share:
        def __init__(self, table):
            self.leave, self.land = send_sem.at[counts[2]], recv_sem.at[counts[0]]
            counts[2] += 1
            counts[0] += 1
            for device in peers:
                pltpu.make_async_remote_copy(
                    src_ref=table.at[dp], dst_ref=table.at[dp], send_sem=self.leave,
                    recv_sem=self.land, device_id=device, device_id_type=MESH,
                ).start()
            self.others = table.at[pl.ds(0, DP - 1)]
            senders.append(self)

        def wait_recv(self):
            pltpu.make_async_copy(self.others, self.others, self.land).wait()

        def finish(self):
            pltpu.make_async_copy(self.others, self.others, self.leave).wait()

    def fetch(src, dst):
        i = counts[1]
        counts[1] += 1
        copy = pltpu.make_async_copy(src, dst, local_sem.at[i])
        copy.start()
        return copy

    in_emb = [fetch(emb_a, emb.at[pl.ds(0, ROWS)]), fetch(emb_b, emb.at[pl.ds(ROWS, ROWS)])]
    in_win = [
        fetch(w_in.at[:, pl.ds(k * TILE, TILE)], win.at[:, pl.ds(k * TILE, TILE)])
        for k in range(WIDE // TILE)
    ]
    in_gs = [fetch(gain, gn_sh.at[pl.ds(0, 1)]), fetch(shift, gn_sh.at[pl.ds(1, 1)])]

    barrier = pltpu.get_barrier_semaphore()
    greeted = peers + [member for _, member in members]
    for device in greeted:
        pl.semaphore_signal(barrier, inc=1, device_id=device, device_id_type=MESH)

    def rows(v):
        return pl.ds(v * ROWS, ROWS)

    def local_moments(values, table, row, cols):
        center = jnp.sum(values, axis=0, keepdims=True) / ROWS
        spread = jnp.sum((values - center) ** 2, axis=0, keepdims=True)
        table[dp, row : row + 1, cols] = center
        table[dp, row + 1 : row + 2, cols] = spread

    def global_moments(table, row, cols):
        centers = table[:, row, cols]
        center = jnp.sum(centers, axis=0, keepdims=True) / DP
        spread = jnp.sum(table[:, row + 1, cols], axis=0, keepdims=True) + ROWS * jnp.sum(
            (centers - center) ** 2, axis=0, keepdims=True
        )
        return center, lax.rsqrt(spread / BATCH + epsilon)

    def first_layer(v):
        in_emb[v].wait()
        for k, copy in enumerate(in_win):
            cols = pl.ds(k * TILE, TILE)
            if v == 0:
                copy.wait()
            hid[v, :, cols] = jnp.dot(emb[rows(v), :], win[:, cols], preferred_element_type=f32)
            local_moments(hid[v, :, cols], st1.at[v], 0, cols)

    def first_norm(v):
        first_layer(v)
        if v == 0:
            waiting.append(fetch(w_out, wout))
            pl.semaphore_wait(barrier, len(greeted))
        exchange = Share(st1.at[v])
        yield
        exchange.wait_recv()
        if v == 0:
            for copy in in_gs:
                copy.wait()

        def tile(cols):
            center, inverse = global_moments(st1.at[v], 0, cols)
            hat = (hid[v, :, cols] - center) * inverse
            hid[v, :, cols] = hat
            inv[v : v + 1, cols] = inverse
            before = gn_sh[0:1, cols] * hat + gn_sh[1:2, cols]
            act[v, ft, :, cols] = jnp.maximum(before, 0.0).astype(bf16)

        column_tiles(tile)

    def project(v, slot, first=False):
        def tile(cols):
            product = jnp.dot(
                act[v, slot], wout[pl.ds(pl.multiple_of(slot * WIDE, WIDE), WIDE), cols],
                preferred_element_type=f32,
            )
            if first:
                out[v, :, cols] = product
            else:
                out[v, :, cols] += product

        column_tiles(tile)

    def gather(buffer, slot, right, left, pair, edge, have):
        send = Sender()
        low, high = pl.ds(0, HALF), pl.ds(HALF, HALF)
        top, bottom = pl.ds(0, edge), pl.ds(ROWS - edge, edge)
        middle = pl.ds(edge, ROWS - 2 * edge)
        split = edge < HALF

        def go_(block, device, part_rows=None):
            ref = buffer.at[block] if part_rows is None else buffer.at[block, part_rows]
            return send(ref, ref, device)

        def arrive(*copies):
            for copy in copies:
                copy.wait_recv()

        a = go_(slot(0, 0), pair)
        b = go_(slot(0, 0), right)
        c = go_(slot(0, 0), left)
        have(0, 0)
        yield
        arrive(a)
        parts = (top, bottom) if split else (None,)
        d = [go_(slot(0, 1), right, part_rows) for part_rows in parts]
        e = [go_(slot(0, 1), left, part_rows) for part_rows in parts[::-1]]
        have(0, 1)
        yield
        late = []
        arrive(b)
        f = go_(slot(-1, 0), right, low)
        if split:
            late.append(go_(slot(-1, 0), pair, middle))
        arrive(c)
        g = go_(slot(1, 0), left, high)
        if split:
            late.append(go_(slot(1, 0), pair, middle))
        yield
        have(-1, 0)
        yield
        have(1, 0)
        yield
        arrive(d[0])
        h = go_(slot(-1, 1), right, top)
        arrive(e[0])
        i = go_(slot(1, 1), left, bottom)
        arrive(*d[1:], *e[1:], *late)
        yield
        have(-1, 1)
        yield
        have(1, 1)
        yield
        arrive(f, g)
        late = [go_(slot(2, 0), pair, middle)] if split else []
        have(2, 0)
        yield
        arrive(h, i, *late)
        have(2, 1)

    def gather_feat(v):
        def have(step, flip):
            if v == 0 and waiting:
                waiting.pop().wait()
            project(v, feat_of(step, flip), first=step == 0 and flip == 0)

        return gather(act.at[v], feat_of, x_right, x_left, y_pair, FEAT_EDGE[v], have)

    def second_norm(v):
        column_tiles(lambda cols: local_moments(out[v, :, cols], st2.at[v], 0, cols))
        exchange = Share(st2.at[v])
        yield
        exchange.wait_recv()

        def tile(cols):
            center, inverse = global_moments(st2.at[v], 0, cols)
            hat = (out[v, :, cols] - center) * inverse
            out[v, :, cols] = hat
            inv[2 + v : 3 + v, cols] = inverse
            nrm[v, dp, :, cols] = hat.astype(bf16)

        column_tiles(tile)

    def inner(v, slot):
        cols = pl.ds(pl.multiple_of(slot * ROWS, ROWS), ROWS)
        part[v, :, cols] = lax.dot_general(
            nrm[v, dp], nrm[v, slot], NT, preferred_element_type=f32
        ).astype(bf16)
        if v == 1:
            corr[pl.ds(slot, 1), :] = jnp.sum(
                nrm[0, slot].astype(f32) * nrm[1, slot].astype(f32), axis=0, keepdims=True
            )

    def gather_dp(v):
        send = Sender()
        cores = []

        def from_core(count):
            for _ in range(count):
                copy, step, flip = cores.pop(0)
                copy.wait_recv()
                inner(v, dp_of(step, flip, 1))

        def have(step, flip):
            slot = dp_of(step, flip)
            cores.append((send(nrm.at[v, slot], nrm.at[v, slot], other), step, flip))
            inner(v, slot)
            if (step, flip) not in ((0, 0), (-1, 0), (-1, 1)):
                from_core(len(cores) if (step, flip) == (2, 1) else len(cores) - 1)

        return gather(nrm.at[v], dp_of, z_right, z_left, y_next, DP_EDGE[v], have)

    def sum_gram(v):
        send = Sender()

        def block(step, flip):
            return pl.ds(pl.multiple_of(feat_of(step, flip) * 16, 16), 16)

        mine = block(0, 0)
        arrivals = [
            send(part.at[v, block(*place)], sum_r.at[v, n], member)
            for n, (place, member) in enumerate(members)
        ]
        yield
        total = part[v, mine, :].astype(f32)
        for n, copy in enumerate(arrivals):
            copy.wait_recv()
            total += sum_r[v, n].astype(f32)
        gram[v, mine, :] = total.astype(bf16)
        arrivals = [
            send(gram.at[v, mine], gram.at[v, mine], member) for _, member in members
        ]
        yield
        for copy in arrivals:
            copy.wait_recv()

    factor = BATCH / 64.0
    coeff = 2.0 * off_weight / (BATCH * BATCH)

    def losses():
        diag = jnp.sum(corr[...], axis=0, keepdims=True) / BATCH
        diag_loss[...] = (1.0 - diag) ** 2 - off_weight * diag**2
        corr[0:1, :] = -2.0 * (1.0 - diag) - 2.0 * off_weight * diag

    def row_losses():
        total = jnp.zeros((ROWS, ROWS), f32)
        for k in range(BATCH // ROWS):
            cols = slice(k * ROWS, (k + 1) * ROWS)
            total += gram[0, :, cols].astype(f32) * gram[1, :, cols].astype(f32)
        total = jnp.sum(total.T, axis=0, keepdims=True)
        row_loss[...] = total / (BATCH * WIDE * FEAT)

    def output_back(v):
        def tile(cols):
            product = jnp.dot(
                gram[1 - v], nrm[v, :, :, cols].reshape(BATCH, TILE), preferred_element_type=f32
            )
            upstream = factor * (
                coeff * product + nrm[1 - v, dp, :, cols].astype(f32) * corr[0:1, cols] / BATCH
            )
            gact[v, :, cols] = upstream
            st3[v, dp, 0:1, cols] = jnp.sum(upstream, axis=0, keepdims=True)
            st3[v, dp, 1:2, cols] = jnp.sum(upstream * out[v, :, cols], axis=0, keepdims=True)

        column_tiles(tile)
        exchange = Share(st3.at[v])
        yield
        exchange.wait_recv()

        def finish(cols):
            up = jnp.sum(st3[v, :, 0, cols], axis=0, keepdims=True) / BATCH
            dot = jnp.sum(st3[v, :, 1, cols], axis=0, keepdims=True) / BATCH
            go[v, :, cols] = (
                inv[2 + v : 3 + v, cols] * (gact[v, :, cols] - up - out[v, :, cols] * dot)
            ).astype(bf16)

        column_tiles(finish)

    def keep(ref):
        def store(cols, value):
            ref[:, cols] = value.astype(bf16)

        return store

    stores = []

    def active_back(v, h):
        send = Sender()
        def block(step, flip, store):
            first = feat_of(step, flip) * WIDE + STARTS[h]

            def tile(cols):
                store(
                    cols,
                    lax.dot_general(
                        go[v], wout[pl.ds(pl.multiple_of(first + cols.start, TILE), TILE), :], NT,
                        preferred_element_type=f32,
                    ),
                )

            column_tiles(tile, PIECES[h])

        edge = BACK_EDGE[v][h]
        top, bottom = pl.ds(0, edge), pl.ds(ROWS - edge, edge)
        middle, between = pl.ds(edge, ROWS - 2 * edge), pl.ds(0, ROWS - 2 * edge)
        mine, here = pl.ds(STARTS[h], PIECES[h]), pl.ds(0, PIECES[h])
        crossed = {}

        def cross(step, ref):
            slot = (2, 1, -1, 0).index(step)
            crossed[step] = send(ref, cross_r.at[v, h, slot, between, here], y_pair)

        def added(step, ref):
            slot = (2, 1, -1, 0).index(step)
            crossed[step].wait_recv()

            def store(cols, value):
                ref[:, cols] = value.astype(bf16)
                ref[middle, cols] = (
                    value[edge : ROWS - edge] + cross_r[v, h, slot, between, cols].astype(f32)
                ).astype(bf16)

            return store

        def far(flip):
            ref = far_s.at[v, h, flip, :, here]
            block(2, flip, keep(ref) if flip else added(2, ref))
            if flip:
                cross(2, ref.at[middle])
            first, second = (top, bottom) if flip else (low, high)
            into = between_half if not flip else pl.ds(0, edge)
            return [
                send(ref.at[first], far_r.at[v, h, flip, 0, into, here], x_right),
                send(ref.at[second], far_r.at[v, h, flip, 1, into, here], x_left),
            ]

        low, high = pl.ds(0, HALF), pl.ds(HALF, HALF)
        between_half = pl.ds(0, HALF)

        def near(flip):
            first, second = (top, bottom) if flip else (low, high)
            copies = []
            for side, step, part_rows, device in ((0, 1, second, x_right), (1, -1, first, x_left)):
                ref = near_s.at[v, h, flip, side, :, here]
                block(step, flip, keep(ref) if flip else added(step, ref))
                copies.append(
                    send(ref.at[part_rows], near_r.at[v, h, flip, side, part_rows, here], device)
                )
                if flip:
                    cross(step, ref.at[middle])
            return copies

        def relay(flip, fars, nears):
            first, second = (top, bottom) if flip else (low, high)
            into = between_half if not flip else pl.ds(0, edge)
            for side, part_rows, device in ((0, first, x_right), (1, second, x_left)):
                fars[side].wait_recv()
                near_s[v, h, flip, side, part_rows, here] = (
                    near_s[v, h, flip, side, part_rows, here].astype(f32)
                    + far_r[v, h, flip, side, into, here].astype(f32)
                ).astype(bf16)
                nears.append(
                    send(
                        near_s.at[v, h, flip, side, part_rows, here],
                        near_r.at[v, h, flip, side, part_rows, here], device,
                    )
                )

        def store_own(cols, value):
            gact[v, :, pl.ds(pl.multiple_of(STARTS[h] + cols.start, TILE), TILE)] = value

        def store_pair(cols, value):
            store_own(cols, value)
            cross_s[v, h, between, cols] = value[edge : ROWS - edge].astype(bf16)

        fars1 = far(1)
        yield
        nears1 = near(1)
        yield
        block(0, 1, store_pair)
        cross(0, cross_s.at[v, h, between, here])
        yield
        fars0 = far(0)
        yield
        relay(1, fars1, nears1)
        yield
        nears0 = near(0)
        yield
        for copy in nears1:
            copy.wait_recv()
        for place, part_rows in ((pl.ds(0, edge), top), (pl.ds(edge, edge), bottom)):
            ys[v, h, place, here] = (
                gact[v, part_rows, mine]
                + near_r[v, h, 1, 0, part_rows, here].astype(f32)
                + near_r[v, h, 1, 1, part_rows, here].astype(f32)
            ).astype(bf16)
        edges = pl.ds(0, 2 * edge)
        last = send(ys.at[v, h, edges, here], yr.at[v, h, edges, here], y_pair)
        yield
        block(0, 0, store_own)
        yield
        relay(0, fars0, nears0)
        yield
        for copy in nears0 + [last, crossed[0]]:
            copy.wait_recv()

    def first_back(h):
        def tile(v, cols):
            edge = BACK_EDGE[v][h]
            full = pl.ds(pl.multiple_of(STARTS[h] + cols.start, TILE), TILE)
            hat = hid[v, :, full]
            grad = (
                gact[v, :, full]
                + near_r[v, h, 0, 0, :, cols].astype(f32)
                + near_r[v, h, 0, 1, :, cols].astype(f32)
                + jnp.concatenate(
                    [
                        yr[v, h, 0:edge, cols],
                        cross_r[v, h, 3, 0 : ROWS - 2 * edge, cols],
                        yr[v, h, edge : 2 * edge, cols],
                    ]
                ).astype(f32)
            )
            before = gn_sh[0:1, full] * hat + gn_sh[1:2, full]
            grad = jnp.where(before > 0, grad, 0.0)
            gact[v, :, full] = grad
            st4[h, dp, 2 * v : 2 * v + 1, cols] = jnp.sum(grad, axis=0, keepdims=True)
            st4[h, dp, 2 * v + 1 : 2 * v + 2, cols] = jnp.sum(grad * hat, axis=0, keepdims=True)

        column_tiles(functools.partial(tile, 1), PIECES[h])
        yield
        column_tiles(functools.partial(tile, 0), PIECES[h])
        exchange = Share(st4.at[h, :, :, pl.ds(0, PIECES[h])])
        yield
        exchange.wait_recv()

        def finish(cols):
            full = pl.ds(pl.multiple_of(STARTS[h] + cols.start, TILE), TILE)
            sums = [jnp.sum(st4[h, :, k, cols], axis=0, keepdims=True) for k in range(4)]
            for v in range(2):
                up, dot = sums[2 * v], sums[2 * v + 1]
                gh[rows(v), full] = (
                    gn_sh[0:1, full] * inv[v : v + 1, full]
                    * (gact[v, :, full] - up / BATCH - hid[v, :, full] * (dot / BATCH))
                ).astype(bf16)
            grad_shift[:, full] = sums[0] + sums[2]
            grad_gain[:, full] = sums[1] + sums[3]

        column_tiles(finish, PIECES[h])

    def transpose_emb():
        for k in range(EMB // ROWS):
            cols = slice(k * ROWS, (k + 1) * ROWS)
            emb_t[cols, :] = emb[:, cols].T

    def last_layer(h):
        send = Sender()
        mine, here = pl.ds(STARTS[h], PIECES[h]), pl.ds(0, PIECES[h])
        low, high = pl.ds(0, OUT // 2), pl.ds(OUT // 2, OUT // 2)

        def product(cols):
            full = pl.ds(pl.multiple_of(STARTS[h] + cols.start, TILE), TILE)
            win[:, full] = jnp.dot(
                emb_t[...], gh[:, full], preferred_element_type=f32
            ).astype(bf16)

        def block(step, flip_y, flip_core):
            target = dp_of(step, flip_y, flip_core)
            return win.at[pl.ds(pl.multiple_of(target * OUT, OUT), OUT), mine]

        column_tiles(product, PIECES[h])
        order = [(2, 1), (1, 1), (-1, 1), (2, 0), (1, 0), (-1, 0), (0, 1), (0, 0)]
        crossing = {}
        for n, (step, flip) in enumerate(order):
            crossing[step, flip] = send(block(step, flip, 1), core_r.at[h, n, :, here], other)
        yield

        def chip_sum(step, flip):
            n = order.index((step, flip))
            crossing[step, flip].wait_recv()
            return block(step, flip, 0)[...].astype(f32) + core_r[h, n, :, here].astype(f32)

        def far(flip):
            far_is[h, flip, :, here] = chip_sum(2, flip).astype(bf16)
            return [
                send(far_is.at[h, flip, low, here], far_ir.at[h, flip, 0, :, here], z_right),
                send(far_is.at[h, flip, high, here], far_ir.at[h, flip, 1, :, here], z_left),
            ]

        def near(flip):
            near_is[h, flip, 0, :, here] = chip_sum(1, flip).astype(bf16)
            a = send(near_is.at[h, flip, 0, high, here], near_ir.at[h, flip, 0, high, here], z_right)
            near_is[h, flip, 1, :, here] = chip_sum(-1, flip).astype(bf16)
            b = send(near_is.at[h, flip, 1, low, here], near_ir.at[h, flip, 1, low, here], z_left)
            return [a, b]

        def relay(flip, fars, nears):
            for side, half, device in ((0, low, z_right), (1, high, z_left)):
                fars[side].wait_recv()
                near_is[h, flip, side, half, here] = (
                    near_is[h, flip, side, half, here].astype(f32) + far_ir[h, flip, side, :, here].astype(f32)
                ).astype(bf16)
                nears.append(
                    send(near_is.at[h, flip, side, half, here], near_ir.at[h, flip, side, half, here], device)
                )

        def line_sum(flip):
            return (
                chip_sum(0, flip)
                + near_ir[h, flip, 0, :, here].astype(f32)
                + near_ir[h, flip, 1, :, here].astype(f32)
            )

        fars1 = far(1)
        nears1 = near(1)
        yield
        fars0 = far(0)
        yield
        relay(1, fars1, nears1)
        yield
        nears0 = near(0)
        yield
        for copy in nears1:
            copy.wait_recv()
        y_is[h, :, here] = line_sum(1).astype(bf16)
        last = send(y_is.at[h, :, here], y_ir.at[h, :, here], y_next)
        yield
        relay(0, fars0, nears0)
        yield
        for copy in nears0 + [last]:
            copy.wait_recv()
        total = line_sum(0)
        gout[:, mine] = total + y_ir[h, :, here].astype(f32)
        stores.append(fetch(gout.at[:, mine], grad_in.at[:, mine]))

    def once(stage, *args):
        stage(*args)
        yield

    first_a, first_b = first_norm(0), first_norm(1)
    feat_a, feat_b = gather_feat(0), gather_feat(1)
    norm_a, norm_b = second_norm(0), second_norm(1)
    dp_a, dp_b = gather_dp(0), gather_dp(1)
    gram_a, gram_b = sum_gram(0), sum_gram(1)
    back_a, back_b = output_back(0), output_back(1)
    act_a0, act_a1, act_b0, act_b1 = (active_back(v, h) for v in range(2) for h in range(2))
    pre_0, pre_1 = first_back(0), first_back(1)
    last_0, last_1 = last_layer(0), last_layer(1)
    loss, row = once(losses), once(row_losses)
    turn = once(transpose_emb)
    order = (
        first_a, first_a, feat_a, feat_a, feat_a, feat_a, first_b, feat_a, first_b, feat_a, feat_b,
        feat_a, feat_a, feat_a, feat_a, norm_a, feat_b, norm_a, dp_a, feat_b, feat_b, feat_b,
        feat_b, feat_b, dp_a, feat_b, feat_b, feat_b, norm_b, dp_a, dp_a, dp_a, dp_a, dp_a, norm_b,
        dp_a, dp_b, dp_a, dp_a, gram_a, dp_b, dp_b, dp_b, dp_b, dp_b, gram_a, dp_b, dp_b, dp_b,
        dp_b, gram_b, gram_a, turn, loss, back_b, gram_b, back_b, act_b0, act_b0, act_b1, act_b0,
        act_b1, act_b1, gram_b, back_a, act_b0, act_b0, act_b1, act_b0, back_a, act_a1, act_a0,
        act_a1, act_b1, act_a1, act_a1, act_a1, act_a0, act_a1, act_b1, act_a0, act_a0, act_b1,
        act_a1, act_b1, act_a0, act_a1, act_b1, act_b0, act_b0, act_a1, act_a0, act_b0, act_a0,
        act_b1, act_a0, act_a0, act_a1, pre_1, pre_1, act_b0, pre_0, act_a0, pre_0, pre_1, last_1,
        pre_0, last_1, last_0, last_1, last_0, last_1, last_0, last_0, last_1, last_0, last_1,
        last_1, last_0, last_0, row, last_1, last_0,
    )
    for stage in order:
        next(stage, None)
    for stage in order:
        for _ in stage:
            raise ValueError()
    for copy in stores:
        copy.wait()
    for sender in senders:
        sender.finish()


def copies(*refs):
    for i in range(5):
        refs[5 + i][...] = refs[i][...]


def scratch():
    v = pltpu.VMEM
    return [
        v((2 * ROWS, EMB), bf16), v((EMB, WIDE), bf16), v((FEAT * WIDE, WIDE), bf16),
        v((2, WIDE), f32), v((4, WIDE), f32), v((2, ROWS, WIDE), f32), v((2, FEAT, ROWS, WIDE), bf16),
        v((2, ROWS, WIDE), f32),
        v((2, DP, 2, WIDE), f32), v((2, DP, 2, WIDE), f32),
        v((2, DP, 2, WIDE), f32), v((2, DP, 4, PIECE), f32),
        v((2, DP, ROWS, WIDE), bf16), v((DP, WIDE), f32),
        v((2, ROWS, BATCH), bf16), v((2, FEAT - 1, 16, BATCH), bf16),
        v((2, ROWS, BATCH), bf16),
        v((2, ROWS, WIDE), bf16),
        v((2, 2, 2, ROWS, PIECE), bf16), v((2, 2, 2, 2, HALF, PIECE), bf16),
        v((2, 2, 2, 2, ROWS, PIECE), bf16), v((2, 2, 2, 2, ROWS, PIECE), bf16),
        v((2, 2, ROWS, PIECE), bf16), v((2, 2, ROWS, PIECE), bf16),
        v((2, 2, HALF, PIECE), bf16), v((2, 2, 4, HALF, PIECE), bf16), v((2, ROWS, WIDE), f32),
        v((2 * ROWS, WIDE), bf16), v((EMB, 2 * ROWS), bf16),
        v((2, 8, OUT, PIECE), bf16),
        v((2, 2, OUT, PIECE), bf16), v((2, 2, 2, OUT // 2, PIECE), bf16),
        v((2, 2, 2, OUT, PIECE), bf16), v((2, 2, 2, OUT, PIECE), bf16),
        v((2, OUT, PIECE), bf16), v((2, OUT, PIECE), bf16), v((OUT, WIDE), f32),
        pltpu.SemaphoreType.DMA((22,)), pltpu.SemaphoreType.DMA((198,)),
        pltpu.SemaphoreType.DMA((11,)),
    ]


def shards(emb_a, emb_b, w_in, w_out, gain, shift):
    anywhere = pl.BlockSpec(memory_space=pl.ANY)
    near = pl.BlockSpec(memory_space=pltpu.VMEM)
    results = pl.pallas_call(
        kernel,
        out_shape=(
            jax.ShapeDtypeStruct((OUT, WIDE), f32),
            jax.ShapeDtypeStruct((1, WIDE), f32),
            jax.ShapeDtypeStruct((1, WIDE), f32),
            jax.ShapeDtypeStruct((1, WIDE), f32),
            jax.ShapeDtypeStruct((1, ROWS), f32),
        ),
        in_specs=[anywhere] * 6,
        out_specs=(anywhere, near, near, near, near),
        scratch_shapes=scratch(),
        compiler_params=pltpu.CompilerParams(
            collective_id=0, has_side_effects=True, vmem_limit_bytes=62 * 2**20
        ),
        cost_estimate=pl.CostEstimate(flops=14 * 10**9, bytes_accessed=24 * 2**20, transcendentals=0),
    )(emb_a, emb_b, w_in, w_out, gain.reshape(1, WIDE), shift.reshape(1, WIDE))
    results = pl.pallas_call(
        copies,
        out_shape=tuple(jax.ShapeDtypeStruct(r.shape, r.dtype) for r in results),
        in_specs=[near] * 5,
        out_specs=(near,) * 5,
    )(*results)
    return (results[0],) + tuple(r.reshape(-1) for r in results[1:])


def solution(mesh):
    return jax.shard_map(
        shards,
        mesh=mesh,
        in_specs=(
            P("dp", None), P("dp", None), P(None, "feat"), P(None, "feat"), P("feat"), P("feat"),
        ),
        out_specs=(P("dp", "feat"), P("feat"), P("feat"), P("feat"), P("dp")),
        check_vma=False,
    )
```

```python
import functools
import math

import jax
import jax.numpy as jnp
from jax import lax
from jax.experimental import pallas as pl
from jax.experimental.pallas import tpu as pltpu
from jax.sharding import PartitionSpec as P

MESH = pl.DeviceIdType.MESH
epsilon = 1e-05
off_weight = 0.0051
BATCH = 2048
ROWS = 128
WIDE = 1024
EMB = 1536
DP = 16
FEAT = 8
OUT = EMB // DP
TILE = 256
PIECES = (512, 512)
STARTS = (0, 512)
PIECE = max(PIECES)
HALF = ROWS // 2
FEAT_EDGE = (HALF, HALF)
DP_EDGE = (HALF, HALF)
BACK_EDGE = ((48, 48), (48, 48))
f32 = jnp.float32
bf16 = jnp.bfloat16
NT = (((1,), (1,)), ((), ()))


def column_tiles(body, width=WIDE, tile=TILE):
    @pl.loop(0, width // tile)
    def _(i):
        body(pl.ds(pl.multiple_of(i * tile, tile), tile))


def kernel(
    emb_a, emb_b, w_in, w_out, gain, shift,
    grad_in, grad_gain, grad_shift, diag_loss, row_loss,
    emb, win, wout, gn_sh, inv, hid, act, out, st1, st2, st3, st4, nrm, corr,
    part, sum_r, gram, go,
    far_s, far_r, near_s, near_r, ys, yr, cross_s, cross_r, gact, gh, emb_t,
    core_r, far_is, far_ir, near_is, near_ir, y_is, y_ir, gout,
    send_sem, recv_sem, local_sem,
):
    dp, ft = lax.axis_index("dp"), lax.axis_index("feat")
    core, z = lax.rem(dp, 2), lax.rem(dp // 2, 4)
    y_lo, x, y_hi = dp // 8, ft // 2, lax.rem(ft, 2)

    def at_x(step):
        return lax.rem(x + step + 4, 4)

    def at_z(step):
        return lax.rem(z + step + 4, 4)

    def feat_of(step, flip=0):
        return at_x(step) * 2 + (y_hi + flip * (1 - 2 * y_hi))

    def dp_of(step, flip_y=0, flip_core=0):
        yy = y_lo + flip_y * (1 - 2 * y_lo)
        return (yy * 4 + at_z(step)) * 2 + (core + flip_core * (1 - 2 * core))

    x_right, x_left, y_pair = (dp, feat_of(1)), (dp, feat_of(-1)), (dp, feat_of(0, 1))
    z_right, z_left = (dp_of(1), ft), (dp_of(-1), ft)
    y_next, other = (dp_of(0, 1), ft), (dp_of(0, 0, 1), ft)
    peers = [(lax.rem(dp + k, DP), ft) for k in range(1, DP)]
    places = [(2, 1), (1, 1), (-1, 1), (2, 0), (0, 1), (1, 0), (-1, 0)]
    members = [(place, (dp, feat_of(*place))) for place in places]

    waiting = []
    counts = [0, 0, 0]

    def size(ref):
        return math.prod(ref.shape) * jnp.dtype(ref.dtype).itemsize

    def all_of(sem, total):
        assert total % (16 * WIDE) == 0
        ref = wout.at[pl.ds(0, total // WIDE), pl.ds(0, WIDE // 2)]
        return pltpu.make_async_copy(ref, ref, sem)

    class Sender:
        def __init__(self):
            self.sem = send_sem.at[counts[2]]
            counts[2] += 1
            self.total = 0
            senders.append(self)

        def __call__(self, src, dst, device):
            i = counts[0]
            counts[0] += 1
            copy = pltpu.make_async_remote_copy(
                src_ref=src, dst_ref=dst, send_sem=self.sem, recv_sem=recv_sem.at[i],
                device_id=device, device_id_type=MESH,
            )
            copy.start()
            self.total += size(src)
            return copy

        def finish(self):
            all_of(self.sem, self.total).wait()

    senders = []

    class Share:
        def __init__(self, table):
            self.leave, self.land = send_sem.at[counts[2]], recv_sem.at[counts[0]]
            counts[2] += 1
            counts[0] += 1
            for device in peers:
                pltpu.make_async_remote_copy(
                    src_ref=table.at[dp], dst_ref=table.at[dp], send_sem=self.leave,
                    recv_sem=self.land, device_id=device, device_id_type=MESH,
                ).start()
            self.others = table.at[pl.ds(0, DP - 1)]
            senders.append(self)

        def wait_recv(self):
            pltpu.make_async_copy(self.others, self.others, self.land).wait()

        def finish(self):
            pltpu.make_async_copy(self.others, self.others, self.leave).wait()

    def fetch(src, dst):
        i = counts[1]
        counts[1] += 1
        copy = pltpu.make_async_copy(src, dst, local_sem.at[i])
        copy.start()
        return copy

    in_emb = [fetch(emb_a, emb.at[pl.ds(0, ROWS)]), fetch(emb_b, emb.at[pl.ds(ROWS, ROWS)])]
    in_win = [
        fetch(w_in.at[:, pl.ds(k * TILE, TILE)], win.at[:, pl.ds(k * TILE, TILE)])
        for k in range(WIDE // TILE)
    ]
    in_gs = [fetch(gain, gn_sh.at[pl.ds(0, 1)]), fetch(shift, gn_sh.at[pl.ds(1, 1)])]

    barrier = pltpu.get_barrier_semaphore()
    greeted = peers + [member for _, member in members]
    for device in greeted:
        pl.semaphore_signal(barrier, inc=1, device_id=device, device_id_type=MESH)

    def rows(v):
        return pl.ds(v * ROWS, ROWS)

    def local_moments(values, table, row, cols):
        center = jnp.sum(values, axis=0, keepdims=True) / ROWS
        spread = jnp.sum((values - center) ** 2, axis=0, keepdims=True)
        table[dp, row : row + 1, cols] = center
        table[dp, row + 1 : row + 2, cols] = spread

    def global_moments(table, row, cols):
        centers = table[:, row, cols]
        center = jnp.sum(centers, axis=0, keepdims=True) / DP
        spread = jnp.sum(table[:, row + 1, cols], axis=0, keepdims=True) + ROWS * jnp.sum(
            (centers - center) ** 2, axis=0, keepdims=True
        )
        return center, lax.rsqrt(spread / BATCH + epsilon)

    def first_layer(v):
        in_emb[v].wait()
        for k, copy in enumerate(in_win):
            cols = pl.ds(k * TILE, TILE)
            if v == 0:
                copy.wait()
            hid[v, :, cols] = jnp.dot(emb[rows(v), :], win[:, cols], preferred_element_type=f32)
            local_moments(hid[v, :, cols], st1.at[v], 0, cols)

    def first_norm(v):
        first_layer(v)
        if v == 0:
            waiting.append(fetch(w_out, wout))
            pl.semaphore_wait(barrier, len(greeted))
        exchange = Share(st1.at[v])
        yield
        exchange.wait_recv()
        if v == 0:
            for copy in in_gs:
                copy.wait()

        def tile(cols):
            center, inverse = global_moments(st1.at[v], 0, cols)
            hat = (hid[v, :, cols] - center) * inverse
            hid[v, :, cols] = hat
            inv[v : v + 1, cols] = inverse
            before = gn_sh[0:1, cols] * hat + gn_sh[1:2, cols]
            act[v, ft, :, cols] = jnp.maximum(before, 0.0).astype(bf16)

        column_tiles(tile)

    def project(v, slot, first=False):
        def tile(cols):
            product = jnp.dot(
                act[v, slot], wout[pl.ds(pl.multiple_of(slot * WIDE, WIDE), WIDE), cols],
                preferred_element_type=f32,
            )
            if first:
                out[v, :, cols] = product
            else:
                out[v, :, cols] += product

        column_tiles(tile)

    def gather(buffer, slot, right, left, pair, edge, have):
        send = Sender()
        low, high = pl.ds(0, HALF), pl.ds(HALF, HALF)
        top, bottom = pl.ds(0, edge), pl.ds(ROWS - edge, edge)
        middle = pl.ds(edge, ROWS - 2 * edge)
        split = edge < HALF

        def go_(block, device, part_rows=None):
            ref = buffer.at[block] if part_rows is None else buffer.at[block, part_rows]
            return send(ref, ref, device)

        def arrive(*copies):
            for copy in copies:
                copy.wait_recv()

        a = go_(slot(0, 0), pair)
        b = go_(slot(0, 0), right)
        c = go_(slot(0, 0), left)
        have(0, 0)
        yield
        arrive(a)
        parts = (top, bottom) if split else (None,)
        d = [go_(slot(0, 1), right, part_rows) for part_rows in parts]
        e = [go_(slot(0, 1), left, part_rows) for part_rows in parts[::-1]]
        have(0, 1)
        yield
        late = []
        arrive(b)
        f = go_(slot(-1, 0), right, low)
        if split:
            late.append(go_(slot(-1, 0), pair, middle))
        arrive(c)
        g = go_(slot(1, 0), left, high)
        if split:
            late.append(go_(slot(1, 0), pair, middle))
        yield
        have(-1, 0)
        yield
        have(1, 0)
        yield
        arrive(d[0])
        h = go_(slot(-1, 1), right, top)
        arrive(e[0])
        i = go_(slot(1, 1), left, bottom)
        arrive(*d[1:], *e[1:], *late)
        yield
        have(-1, 1)
        yield
        have(1, 1)
        yield
        arrive(f, g)
        late = [go_(slot(2, 0), pair, middle)] if split else []
        have(2, 0)
        yield
        arrive(h, i, *late)
        have(2, 1)

    def gather_feat(v):
        def have(step, flip):
            if v == 0 and waiting:
                waiting.pop().wait()
            project(v, feat_of(step, flip), first=step == 0 and flip == 0)

        return gather(act.at[v], feat_of, x_right, x_left, y_pair, FEAT_EDGE[v], have)

    def second_norm(v):
        column_tiles(lambda cols: local_moments(out[v, :, cols], st2.at[v], 0, cols))
        exchange = Share(st2.at[v])
        yield
        exchange.wait_recv()

        def tile(cols):
            center, inverse = global_moments(st2.at[v], 0, cols)
            hat = (out[v, :, cols] - center) * inverse
            out[v, :, cols] = hat
            inv[2 + v : 3 + v, cols] = inverse
            nrm[v, dp, :, cols] = hat.astype(bf16)

        column_tiles(tile)

    def inner(v, slot):
        cols = pl.ds(pl.multiple_of(slot * ROWS, ROWS), ROWS)
        part[v, :, cols] = lax.dot_general(
            nrm[v, dp], nrm[v, slot], NT, preferred_element_type=f32
        ).astype(bf16)
        if v == 1:
            corr[pl.ds(slot, 1), :] = jnp.sum(
                nrm[0, slot].astype(f32) * nrm[1, slot].astype(f32), axis=0, keepdims=True
            )

    def gather_dp(v):
        send = Sender()
        cores = []

        def from_core(count):
            for _ in range(count):
                copy, step, flip = cores.pop(0)
                copy.wait_recv()
                inner(v, dp_of(step, flip, 1))

        def have(step, flip):
            slot = dp_of(step, flip)
            cores.append((send(nrm.at[v, slot], nrm.at[v, slot], other), step, flip))
            inner(v, slot)
            if (step, flip) not in ((0, 0), (-1, 0), (-1, 1)):
                from_core(len(cores) if (step, flip) == (2, 1) else len(cores) - 1)

        return gather(nrm.at[v], dp_of, z_right, z_left, y_next, DP_EDGE[v], have)

    def sum_gram(v):
        send = Sender()

        def block(step, flip):
            return pl.ds(pl.multiple_of(feat_of(step, flip) * 16, 16), 16)

        mine = block(0, 0)
        arrivals = [
            send(part.at[v, block(*place)], sum_r.at[v, n], member)
            for n, (place, member) in enumerate(members)
        ]
        yield
        total = part[v, mine, :].astype(f32)
        for n, copy in enumerate(arrivals):
            copy.wait_recv()
            total += sum_r[v, n].astype(f32)
        gram[v, mine, :] = total.astype(bf16)
        arrivals = [
            send(gram.at[v, mine], gram.at[v, mine], member) for _, member in members
        ]
        yield
        for copy in arrivals:
            copy.wait_recv()

    factor = BATCH / 64.0
    coeff = 2.0 * off_weight / (BATCH * BATCH)

    def losses():
        diag = jnp.sum(corr[...], axis=0, keepdims=True) / BATCH
        diag_loss[...] = (1.0 - diag) ** 2 - off_weight * diag**2
        corr[0:1, :] = -2.0 * (1.0 - diag) - 2.0 * off_weight * diag

    def row_losses():
        total = jnp.zeros((ROWS, ROWS), f32)
        for k in range(BATCH // ROWS):
            cols = slice(k * ROWS, (k + 1) * ROWS)
            total += gram[0, :, cols].astype(f32) * gram[1, :, cols].astype(f32)
        total = jnp.sum(total.T, axis=0, keepdims=True)
        row_loss[...] = total / (BATCH * WIDE * FEAT)

    def output_back(v):
        def tile(cols):
            product = jnp.dot(
                gram[1 - v], nrm[v, :, :, cols].reshape(BATCH, TILE), preferred_element_type=f32
            )
            upstream = factor * (
                coeff * product + nrm[1 - v, dp, :, cols].astype(f32) * corr[0:1, cols] / BATCH
            )
            gact[v, :, cols] = upstream
            st3[v, dp, 0:1, cols] = jnp.sum(upstream, axis=0, keepdims=True)
            st3[v, dp, 1:2, cols] = jnp.sum(upstream * out[v, :, cols], axis=0, keepdims=True)

        column_tiles(tile)
        exchange = Share(st3.at[v])
        yield
        exchange.wait_recv()

        def finish(cols):
            up = jnp.sum(st3[v, :, 0, cols], axis=0, keepdims=True) / BATCH
            dot = jnp.sum(st3[v, :, 1, cols], axis=0, keepdims=True) / BATCH
            go[v, :, cols] = (
                inv[2 + v : 3 + v, cols] * (gact[v, :, cols] - up - out[v, :, cols] * dot)
            ).astype(bf16)

        column_tiles(finish)

    def keep(ref):
        def store(cols, value):
            ref[:, cols] = value.astype(bf16)

        return store

    stores = []

    def active_back(v, h):
        send = Sender()
        def block(step, flip, store):
            first = feat_of(step, flip) * WIDE + STARTS[h]

            def tile(cols):
                store(
                    cols,
                    lax.dot_general(
                        go[v], wout[pl.ds(pl.multiple_of(first + cols.start, TILE), TILE), :], NT,
                        preferred_element_type=f32,
                    ),
                )

            column_tiles(tile, PIECES[h])

        edge = BACK_EDGE[v][h]
        top, bottom = pl.ds(0, edge), pl.ds(ROWS - edge, edge)
        middle, between = pl.ds(edge, ROWS - 2 * edge), pl.ds(0, ROWS - 2 * edge)
        mine, here = pl.ds(STARTS[h], PIECES[h]), pl.ds(0, PIECES[h])
        crossed = {}

        def cross(step, ref):
            slot = (2, 1, -1, 0).index(step)
            crossed[step] = send(ref, cross_r.at[v, h, slot, between, here], y_pair)

        def added(step, ref):
            slot = (2, 1, -1, 0).index(step)
            crossed[step].wait_recv()

            def store(cols, value):
                ref[:, cols] = value.astype(bf16)
                ref[middle, cols] = (
                    value[edge : ROWS - edge] + cross_r[v, h, slot, between, cols].astype(f32)
                ).astype(bf16)

            return store

        def far(flip):
            ref = far_s.at[v, h, flip, :, here]
            block(2, flip, keep(ref) if flip else added(2, ref))
            if flip:
                cross(2, ref.at[middle])
            first, second = (top, bottom) if flip else (low, high)
            into = between_half if not flip else pl.ds(0, edge)
            return [
                send(ref.at[first], far_r.at[v, h, flip, 0, into, here], x_right),
                send(ref.at[second], far_r.at[v, h, flip, 1, into, here], x_left),
            ]

        low, high = pl.ds(0, HALF), pl.ds(HALF, HALF)
        between_half = pl.ds(0, HALF)

        def near(flip):
            first, second = (top, bottom) if flip else (low, high)
            copies = []
            for side, step, part_rows, device in ((0, 1, second, x_right), (1, -1, first, x_left)):
                ref = near_s.at[v, h, flip, side, :, here]
                block(step, flip, keep(ref) if flip else added(step, ref))
                copies.append(
                    send(ref.at[part_rows], near_r.at[v, h, flip, side, part_rows, here], device)
                )
                if flip:
                    cross(step, ref.at[middle])
            return copies

        def relay(flip, fars, nears):
            first, second = (top, bottom) if flip else (low, high)
            into = between_half if not flip else pl.ds(0, edge)
            for side, part_rows, device in ((0, first, x_right), (1, second, x_left)):
                fars[side].wait_recv()
                near_s[v, h, flip, side, part_rows, here] = (
                    near_s[v, h, flip, side, part_rows, here].astype(f32)
                    + far_r[v, h, flip, side, into, here].astype(f32)
                ).astype(bf16)
                nears.append(
                    send(
                        near_s.at[v, h, flip, side, part_rows, here],
                        near_r.at[v, h, flip, side, part_rows, here], device,
                    )
                )

        def store_own(cols, value):
            gact[v, :, pl.ds(pl.multiple_of(STARTS[h] + cols.start, TILE), TILE)] = value

        def store_pair(cols, value):
            store_own(cols, value)
            cross_s[v, h, between, cols] = value[edge : ROWS - edge].astype(bf16)

        fars1 = far(1)
        yield
        nears1 = near(1)
        yield
        block(0, 1, store_pair)
        cross(0, cross_s.at[v, h, between, here])
        yield
        fars0 = far(0)
        yield
        relay(1, fars1, nears1)
        yield
        nears0 = near(0)
        yield
        for copy in nears1:
            copy.wait_recv()
        for place, part_rows in ((pl.ds(0, edge), top), (pl.ds(edge, edge), bottom)):
            ys[v, h, place, here] = (
                gact[v, part_rows, mine]
                + near_r[v, h, 1, 0, part_rows, here].astype(f32)
                + near_r[v, h, 1, 1, part_rows, here].astype(f32)
            ).astype(bf16)
        edges = pl.ds(0, 2 * edge)
        last = send(ys.at[v, h, edges, here], yr.at[v, h, edges, here], y_pair)
        yield
        block(0, 0, store_own)
        yield
        relay(0, fars0, nears0)
        yield
        for copy in nears0 + [last, crossed[0]]:
            copy.wait_recv()

    def first_back(h):
        def tile(v, cols):
            edge = BACK_EDGE[v][h]
            full = pl.ds(pl.multiple_of(STARTS[h] + cols.start, TILE), TILE)
            hat = hid[v, :, full]
            grad = (
                gact[v, :, full]
                + near_r[v, h, 0, 0, :, cols].astype(f32)
                + near_r[v, h, 0, 1, :, cols].astype(f32)
                + jnp.concatenate(
                    [
                        yr[v, h, 0:edge, cols],
                        cross_r[v, h, 3, 0 : ROWS - 2 * edge, cols],
                        yr[v, h, edge : 2 * edge, cols],
                    ]
                ).astype(f32)
            )
            before = gn_sh[0:1, full] * hat + gn_sh[1:2, full]
            grad = jnp.where(before > 0, grad, 0.0)
            gact[v, :, full] = grad
            st4[h, dp, 2 * v : 2 * v + 1, cols] = jnp.sum(grad, axis=0, keepdims=True)
            st4[h, dp, 2 * v + 1 : 2 * v + 2, cols] = jnp.sum(grad * hat, axis=0, keepdims=True)

        column_tiles(functools.partial(tile, 1), PIECES[h])
        yield
        column_tiles(functools.partial(tile, 0), PIECES[h])
        exchange = Share(st4.at[h, :, :, pl.ds(0, PIECES[h])])
        yield
        exchange.wait_recv()

        def finish(cols):
            full = pl.ds(pl.multiple_of(STARTS[h] + cols.start, TILE), TILE)
            sums = [jnp.sum(st4[h, :, k, cols], axis=0, keepdims=True) for k in range(4)]
            for v in range(2):
                up, dot = sums[2 * v], sums[2 * v + 1]
                gh[rows(v), full] = (
                    gn_sh[0:1, full] * inv[v : v + 1, full]
                    * (gact[v, :, full] - up / BATCH - hid[v, :, full] * (dot / BATCH))
                ).astype(bf16)
            grad_shift[:, full] = sums[0] + sums[2]
            grad_gain[:, full] = sums[1] + sums[3]

        column_tiles(finish, PIECES[h])

    def transpose_emb():
        for k in range(EMB // ROWS):
            cols = slice(k * ROWS, (k + 1) * ROWS)
            emb_t[cols, :] = emb[:, cols].T

    def last_layer(h):
        send = Sender()
        mine, here = pl.ds(STARTS[h], PIECES[h]), pl.ds(0, PIECES[h])
        low, high = pl.ds(0, OUT // 2), pl.ds(OUT // 2, OUT // 2)

        def product(cols):
            full = pl.ds(pl.multiple_of(STARTS[h] + cols.start, TILE), TILE)
            win[:, full] = jnp.dot(
                emb_t[...], gh[:, full], preferred_element_type=f32
            ).astype(bf16)

        def block(step, flip_y, flip_core):
            target = dp_of(step, flip_y, flip_core)
            return win.at[pl.ds(pl.multiple_of(target * OUT, OUT), OUT), mine]

        column_tiles(product, PIECES[h])
        order = [(2, 1), (1, 1), (-1, 1), (2, 0), (1, 0), (-1, 0), (0, 1), (0, 0)]
        crossing = {}
        for n, (step, flip) in enumerate(order):
            crossing[step, flip] = send(block(step, flip, 1), core_r.at[h, n, :, here], other)
        yield

        def chip_sum(step, flip):
            n = order.index((step, flip))
            crossing[step, flip].wait_recv()
            return block(step, flip, 0)[...].astype(f32) + core_r[h, n, :, here].astype(f32)

        def far(flip):
            far_is[h, flip, :, here] = chip_sum(2, flip).astype(bf16)
            return [
                send(far_is.at[h, flip, low, here], far_ir.at[h, flip, 0, :, here], z_right),
                send(far_is.at[h, flip, high, here], far_ir.at[h, flip, 1, :, here], z_left),
            ]

        def near(flip):
            near_is[h, flip, 0, :, here] = chip_sum(1, flip).astype(bf16)
            a = send(near_is.at[h, flip, 0, high, here], near_ir.at[h, flip, 0, high, here], z_right)
            near_is[h, flip, 1, :, here] = chip_sum(-1, flip).astype(bf16)
            b = send(near_is.at[h, flip, 1, low, here], near_ir.at[h, flip, 1, low, here], z_left)
            return [a, b]

        def relay(flip, fars, nears):
            for side, half, device in ((0, low, z_right), (1, high, z_left)):
                fars[side].wait_recv()
                near_is[h, flip, side, half, here] = (
                    near_is[h, flip, side, half, here].astype(f32) + far_ir[h, flip, side, :, here].astype(f32)
                ).astype(bf16)
                nears.append(
                    send(near_is.at[h, flip, side, half, here], near_ir.at[h, flip, side, half, here], device)
                )

        def line_sum(flip):
            return (
                chip_sum(0, flip)
                + near_ir[h, flip, 0, :, here].astype(f32)
                + near_ir[h, flip, 1, :, here].astype(f32)
            )

        fars1 = far(1)
        nears1 = near(1)
        yield
        fars0 = far(0)
        yield
        relay(1, fars1, nears1)
        yield
        nears0 = near(0)
        yield
        for copy in nears1:
            copy.wait_recv()
        y_is[h, :, here] = line_sum(1).astype(bf16)
        last = send(y_is.at[h, :, here], y_ir.at[h, :, here], y_next)
        yield
        relay(0, fars0, nears0)
        yield
        for copy in nears0 + [last]:
            copy.wait_recv()
        total = line_sum(0)
        gout[:, mine] = total + y_ir[h, :, here].astype(f32)
        stores.append(fetch(gout.at[:, mine], grad_in.at[:, mine]))

    def once(stage, *args):
        stage(*args)
        yield

    first_a, first_b = first_norm(0), first_norm(1)
    feat_a, feat_b = gather_feat(0), gather_feat(1)
    norm_a, norm_b = second_norm(0), second_norm(1)
    dp_a, dp_b = gather_dp(0), gather_dp(1)
    gram_a, gram_b = sum_gram(0), sum_gram(1)
    back_a, back_b = output_back(0), output_back(1)
    act_a0, act_a1, act_b0, act_b1 = (active_back(v, h) for v in range(2) for h in range(2))
    pre_0, pre_1 = first_back(0), first_back(1)
    last_0, last_1 = last_layer(0), last_layer(1)
    loss, row = once(losses), once(row_losses)
    turn = once(transpose_emb)
    order = (
        first_a, first_a, feat_a, feat_a, first_b, feat_a, feat_a, first_b, feat_a, feat_a, feat_a,
        feat_b, feat_a, feat_a, feat_a, norm_a, feat_b, norm_a, dp_a, feat_b, feat_b, feat_b, turn,
        feat_b, feat_b, dp_a, feat_b, feat_b, feat_b, norm_b, dp_a, dp_a, dp_a, dp_a, dp_a, norm_b,
        dp_b, dp_a, dp_a, dp_a, gram_a, dp_b, dp_b, dp_b, dp_b, dp_b, dp_b, gram_a, dp_b, dp_b,
        dp_b, gram_b, gram_a, loss, back_b, gram_b, back_b, act_b1, act_b1, act_b1, act_b0, act_b0,
        act_b0, gram_b, act_b1, back_a, act_b0, act_b0, act_b0, back_a, act_a1, act_b1, act_a0,
        act_a0, act_a0, act_a1, act_a1, act_b0, act_a1, act_b0, act_a0, act_a0, act_b0, act_b1,
        act_b1, act_a1, act_b1, act_a0, act_b0, act_a0, act_a0, act_a0, act_a1, act_a1, act_a1,
        act_b1, act_a1, act_a0, pre_0, pre_0, act_b1, pre_1, act_a1, pre_1, pre_0, last_0, pre_1,
        last_0, last_1, last_0, last_1, last_0, last_1, last_1, last_0, last_1, last_0, last_0,
        last_1, last_1, row, last_0, last_1,
    )
    for stage in order:
        next(stage, None)
    for stage in order:
        for _ in stage:
            raise ValueError()
    for copy in stores:
        copy.wait()
    for sender in senders:
        sender.finish()


def copies(*refs):
    for i in range(5):
        refs[5 + i][...] = refs[i][...]


def scratch():
    v = pltpu.VMEM
    return [
        v((2 * ROWS, EMB), bf16), v((EMB, WIDE), bf16), v((FEAT * WIDE, WIDE), bf16),
        v((2, WIDE), f32), v((4, WIDE), f32), v((2, ROWS, WIDE), f32), v((2, FEAT, ROWS, WIDE), bf16),
        v((2, ROWS, WIDE), f32),
        v((2, DP, 2, WIDE), f32), v((2, DP, 2, WIDE), f32),
        v((2, DP, 2, WIDE), f32), v((2, DP, 4, PIECE), f32),
        v((2, DP, ROWS, WIDE), bf16), v((DP, WIDE), f32),
        v((2, ROWS, BATCH), bf16), v((2, FEAT - 1, 16, BATCH), bf16),
        v((2, ROWS, BATCH), bf16),
        v((2, ROWS, WIDE), bf16),
        v((2, 2, 2, ROWS, PIECE), bf16), v((2, 2, 2, 2, HALF, PIECE), bf16),
        v((2, 2, 2, 2, ROWS, PIECE), bf16), v((2, 2, 2, 2, ROWS, PIECE), bf16),
        v((2, 2, ROWS, PIECE), bf16), v((2, 2, ROWS, PIECE), bf16),
        v((2, 2, HALF, PIECE), bf16), v((2, 2, 4, HALF, PIECE), bf16), v((2, ROWS, WIDE), f32),
        v((2 * ROWS, WIDE), bf16), v((EMB, 2 * ROWS), bf16),
        v((2, 8, OUT, PIECE), bf16),
        v((2, 2, OUT, PIECE), bf16), v((2, 2, 2, OUT // 2, PIECE), bf16),
        v((2, 2, 2, OUT, PIECE), bf16), v((2, 2, 2, OUT, PIECE), bf16),
        v((2, OUT, PIECE), bf16), v((2, OUT, PIECE), bf16), v((OUT, WIDE), f32),
        pltpu.SemaphoreType.DMA((22,)), pltpu.SemaphoreType.DMA((198,)),
        pltpu.SemaphoreType.DMA((11,)),
    ]


def shards(emb_a, emb_b, w_in, w_out, gain, shift):
    anywhere = pl.BlockSpec(memory_space=pl.ANY)
    near = pl.BlockSpec(memory_space=pltpu.VMEM)
    results = pl.pallas_call(
        kernel,
        out_shape=(
            jax.ShapeDtypeStruct((OUT, WIDE), f32),
            jax.ShapeDtypeStruct((1, WIDE), f32),
            jax.ShapeDtypeStruct((1, WIDE), f32),
            jax.ShapeDtypeStruct((1, WIDE), f32),
            jax.ShapeDtypeStruct((1, ROWS), f32),
        ),
        in_specs=[anywhere] * 6,
        out_specs=(anywhere, near, near, near, near),
        scratch_shapes=scratch(),
        compiler_params=pltpu.CompilerParams(
            collective_id=0, has_side_effects=True, vmem_limit_bytes=62 * 2**20
        ),
        cost_estimate=pl.CostEstimate(flops=14 * 10**9, bytes_accessed=24 * 2**20, transcendentals=0),
    )(emb_a, emb_b, w_in, w_out, gain.reshape(1, WIDE), shift.reshape(1, WIDE))
    results = pl.pallas_call(
        copies,
        out_shape=tuple(jax.ShapeDtypeStruct(r.shape, r.dtype) for r in results),
        in_specs=[near] * 5,
        out_specs=(near,) * 5,
    )(*results)
    return (results[0],) + tuple(r.reshape(-1) for r in results[1:])


def solution(mesh):
    return jax.shard_map(
        shards,
        mesh=mesh,
        in_specs=(
            P("dp", None), P("dp", None), P(None, "feat"), P(None, "feat"), P("feat"), P("feat"),
        ),
        out_specs=(P("dp", "feat"), P("feat"), P("feat"), P("feat"), P("dp")),
        check_vma=False,
    )
```
